32 devices in a mesh: dp: 8 (over y, x, core), mp: 4 (over z).
Axes of the slice: x: 2, y: 2, z: 4, core: 2. Of those that a mesh axis runs over, the one named last changes fastest.
Arguments:
- tokens: bfloat16 [4096, 6144], P('dp', 'mp'), may hold values from -6 to 6
- ln_gain: float32 [6144], replicated, may hold values from 0.1 to 1.9
- w_qkv: bfloat16 [6144, 9216], P('dp', 'mp'), may hold values from -0.078125 to 0.078125
- q_gain: float32 [128], replicated, may hold values from 0.5 to 12
- k_gain: float32 [128], replicated, may hold values from 0.5 to 12
Outputs:
- attended: bfloat16 [4096, 3072], P('dp', 'mp')
The draws below stay inside these ranges and needn't reach their ends.
All inputs are finite; a program needn't handle non-finite values.
Results may differ from the reference program's by a relative error of at most 0.008.
The reference program's roundings to bfloat16 on the way count: a program that leaves them out, or rounds other values in their place, can miss the bound.
Values may be sent and summed in bfloat16 or wider, within the bound.
No kernel may reach another device: no remote copies, remote signals or barrier semaphores. Data moves between devices by JAX's collectives and lax.ppermute only.
A program may use at most 128 MiB of HBM per device.

```python
import math
import jax
import jax.numpy as jnp
from jax import lax

D = 6144
HEADS = 24
HD = 128
SEQ = 256
IMG_DEV = 2
TOKENS = 4096
N_DP = 8


def gain_values(key, low, high):
    uniform_values = jax.random.uniform(key, (HD,), jnp.float32)
    return jnp.exp(math.log(low) + uniform_values * (math.log(high) - math.log(low)))


def draw_q_gain(key, part):
    key = jax.random.fold_in(key, 11)
    return gain_values(key, 0.5, 2.0)


def draw_k_gain(key, part):
    key = jax.random.fold_in(key, 12)
    return gain_values(key, 0.5, 2.0)


def level_of(key, extent, split, least, high):
    def one(dim, shards_of):
        heights = jax.random.uniform(jax.random.fold_in(jax.random.fold_in(key, 6), dim), (shards_of,), jnp.float32, least / len(split), high / len(split))
        return jnp.repeat(jnp.exp(heights), extent[dim] // shards_of).reshape((-1,) + (1,) * (len(extent) - dim - 1))

    factor_of = one(*split[0])
    for cut in split[1:]:
        factor_of = factor_of * one(*cut)
    return factor_of


def gaussian(stream_key, dims, spread, most, cuts=(), dtype=jnp.bfloat16):
    values = spread * jax.random.normal(stream_key, dims, jnp.float32)
    if cuts:
        values = values * level_of(stream_key, dims, cuts, -0.22, 0.18)
    return jnp.clip(values, -most, most).astype(dtype)


def setup_inputs(seed: int = 0) -> dict:
    arg_keys = jax.random.split(jax.random.key(seed), 6)
    tokens = gaussian(arg_keys[0], (TOKENS, D), 1.0, 6.0, ((0, 8), (1, 4)))
    ln_gain = jnp.clip(1.0 + 0.18 * jax.random.normal(arg_keys[1], (D,), jnp.float32), 0.1, 1.9)
    w_qkv = gaussian(arg_keys[2], (D, 3 * HEADS * HD), D ** -0.5, 0.078125, ((0, 8), (1, 4)))
    q_gain = draw_q_gain(jax.random.fold_in(arg_keys[5], 71), 0)
    k_gain = draw_k_gain(jax.random.fold_in(arg_keys[5], 71), 0)
    return dict(tokens=tokens, ln_gain=ln_gain, w_qkv=w_qkv, q_gain=q_gain, k_gain=k_gain)


eps = 1e-06

def layer_norm(values, gain):
    mean = lax.optimization_barrier(jnp.mean(values, axis=-1, keepdims=True))
    square = lax.optimization_barrier(jnp.mean(values * values, axis=-1, keepdims=True))
    return (values - mean) * lax.rsqrt(square - mean * mean + eps) * gain

def reference(tokens, ln_gain, w_qkv, q_gain, k_gain):
    normed = layer_norm(tokens.astype(jnp.float32), ln_gain).astype(jnp.bfloat16)
    images = normed.reshape(IMG_DEV * N_DP, SEQ, D)
    scale = 1.0 / HD ** 0.5

    def one_image(image):
        proj = jnp.dot(image, w_qkv, preferred_element_type=jnp.float32).reshape(SEQ, HEADS, 3, HD)
        query = layer_norm(proj[:, :, 0], q_gain).astype(jnp.bfloat16)
        keyed = layer_norm(proj[:, :, 1], k_gain).astype(jnp.bfloat16)
        value = proj[:, :, 2].astype(jnp.bfloat16)
        scores = jnp.einsum('qhd,khd->hqk', query.astype(jnp.float32), keyed.astype(jnp.float32)) * scale
        probs = jax.nn.softmax(scores, axis=-1).astype(jnp.bfloat16)
        result = jnp.einsum('hqk,khd->qhd', probs.astype(jnp.float32), value.astype(jnp.float32))
        return result.astype(jnp.bfloat16).reshape(SEQ, HEADS * HD)
    return lax.map(one_image, images).reshape(IMG_DEV * N_DP * SEQ, HEADS * HD)
```

```python
import functools

import jax
import jax.numpy as jnp
from jax import lax
from jax.experimental import pallas as pl
from jax.experimental.pallas import tpu as pltpu
from jax.sharding import PartitionSpec as P

HD = 128
SEQ = 256
BLOCKS = 8

eps = 1e-06


def norm_last(values, gain):
    mean = jnp.mean(values, axis=-1, keepdims=True)
    square = jnp.mean(values * values, axis=-1, keepdims=True)
    return (values - mean) * lax.rsqrt(square - mean * mean + eps) * gain


def norm_kernel(x_ref, gain_ref, out_ref):
    shards, rows, width = x_ref.shape
    depth = out_ref.shape[2]
    total = jnp.zeros((rows, 1), jnp.float32)
    squares = jnp.zeros((rows, 1), jnp.float32)
    for s in range(shards):
        x = x_ref[s].astype(jnp.float32)
        total += jnp.sum(x, axis=-1, keepdims=True)
        squares += jnp.sum(x * x, axis=-1, keepdims=True)
    mean = total / (shards * width)
    scale = lax.rsqrt(squares / (shards * width) - mean * mean + eps)
    for s in range(shards):
        x = x_ref[s].astype(jnp.float32)
        y = ((x - mean) * scale * gain_ref[:, s * width : (s + 1) * width]).astype(jnp.bfloat16)
        first = s * width
        done = 0
        while done < width:
            block, lane = divmod(first + done, depth)
            take = min(depth - lane, width - done)
            out_ref[block, :, lane : lane + take] = y[:, done : done + take]
            done += take


def normalize(whole, gain):
    shards, rows, width = whole.shape
    depth = shards * width // BLOCKS
    step = 64
    return pl.pallas_call(
        norm_kernel,
        grid=(rows // step,),
        in_specs=[
            pl.BlockSpec((shards, step, width), lambda r: (0, r, 0)),
            pl.BlockSpec((1, shards * width), lambda r: (0, 0)),
        ],
        out_specs=pl.BlockSpec((BLOCKS, step, depth), lambda r: (0, r, 0)),
        out_shape=jax.ShapeDtypeStruct((BLOCKS, rows, depth), jnp.bfloat16),
        compiler_params=pltpu.CompilerParams(vmem_limit_bytes=32 * 2**20),
        cost_estimate=pl.CostEstimate(
            flops=8 * rows * shards * width, bytes_accessed=4 * rows * shards * width, transcendentals=0
        ),
    )(whole, gain.reshape(1, -1))


def heads_kernel(plan, heads, order_ref, normed_ref, qg_ref, kg_ref, *refs):
    sources = refs[:-6]
    out_ref, x_all, w_all, acc, x_sem, w_sem = refs[-6:]
    for m in range(BLOCKS):
        for source, row, col, block, at, rows in plan:
            if block == m:
                pltpu.make_async_copy(
                    sources[source].at[pl.ds(row, rows), pl.ds(col, w_all.shape[2])],
                    w_all.at[m, pl.ds(at, rows)],
                    w_sem.at[m],
                ).start()
        pltpu.make_async_copy(normed_ref.at[order_ref[m]], x_all.at[m], x_sem.at[m]).start()

    def product(m):
        pltpu.make_async_copy(w_all.at[m], w_all.at[m], w_sem.at[m]).wait()
        pltpu.make_async_copy(x_all.at[m], x_all.at[m], x_sem.at[m]).wait()
        return jnp.dot(x_all[m], w_all[m], preferred_element_type=jnp.float32)

    acc[...] = product(0)

    @pl.loop(1, BLOCKS)
    def _(m):
        acc[...] += product(m)

    scale = 1.0 / HD**0.5
    for h in range(heads):
        base = 3 * HD * h
        query = norm_last(acc[:, base : base + HD], qg_ref[...]).astype(jnp.bfloat16)
        keyed = norm_last(acc[:, base + HD : base + 2 * HD], kg_ref[...]).astype(jnp.bfloat16)
        value = acc[:, base + 2 * HD : base + 3 * HD].astype(jnp.bfloat16)
        for i in range(acc.shape[0] // SEQ):
            rows = slice(i * SEQ, (i + 1) * SEQ)
            scores = lax.dot_general(
                query[rows], keyed[rows], (((1,), (1,)), ((), ())), preferred_element_type=jnp.float32
            ) * scale
            e = jnp.exp(scores - jnp.max(scores, axis=-1, keepdims=True))
            probs = (e / jnp.sum(e, axis=-1, keepdims=True)).astype(jnp.bfloat16)
            out_ref[rows, h * HD : (h + 1) * HD] = jnp.dot(
                probs, value[rows], preferred_element_type=jnp.float32
            ).astype(jnp.bfloat16)


def attend(order, normed, sources, plan, q_gain, k_gain, heads):
    _, rows, depth = normed.shape
    cols = 3 * HD * heads
    anywhere = pl.BlockSpec(memory_space=pl.ANY)
    inside = pl.BlockSpec(memory_space=pltpu.VMEM)
    return pl.pallas_call(
        functools.partial(heads_kernel, plan, heads),
        in_specs=[pl.BlockSpec(memory_space=pltpu.SMEM), anywhere, inside, inside] + [anywhere] * len(sources),
        out_specs=inside,
        out_shape=jax.ShapeDtypeStruct((rows, HD * heads), jnp.bfloat16),
        scratch_shapes=[
            pltpu.VMEM((BLOCKS, rows, depth), jnp.bfloat16),
            pltpu.VMEM((BLOCKS, depth, cols), jnp.bfloat16),
            pltpu.VMEM((rows, cols), jnp.float32),
            pltpu.SemaphoreType.DMA((BLOCKS,)),
            pltpu.SemaphoreType.DMA((BLOCKS,)),
        ],
        compiler_params=pltpu.CompilerParams(vmem_limit_bytes=40 * 2**20),
        cost_estimate=pl.CostEstimate(
            flops=2 * rows * BLOCKS * depth * cols,
            bytes_accessed=2 * BLOCKS * depth * (cols + rows),
            transcendentals=heads * rows * SEQ,
        ),
    )(order, normed, q_gain.reshape(1, HD), k_gain.reshape(1, HD), *sources)


def square_groups(w, sizes):
    def swap(values, bit):
        return lax.ppermute(values, "dp", [(i, i ^ bit) for i in range(8)])

    half = w.shape[0] // 2
    top, low = w[:half], w[half:]
    x_low, y_top = swap(low, 2), swap(top, 4)
    x_top, y_low = swap(top, 2), swap(low, 4)
    near = [w, swap(w, 1)]
    sides = [x_top, x_low, y_top, y_low]
    sides += [swap(s, 1) for s in sides]
    groups = []
    col = 0
    for heads in sizes:
        cols = 3 * HD * heads
        d_top = swap(y_top[:, col : col + cols], 2)
        d_low = swap(x_low[:, col : col + cols], 4)
        far = [d_top, d_low, swap(d_top, 1), swap(d_low, 1)]
        plan = [(0, 0, col, 0, 0, 2 * half), (1, 0, col, 1, 0, 2 * half)]
        for n, block in enumerate((2, 4, 3, 5)):
            plan += [(2 + 2 * n, 0, col, block, 0, half), (3 + 2 * n, 0, col, block, half, half)]
        for n, block in enumerate((6, 7)):
            plan += [(10 + 2 * n, 0, 0, block, 0, half), (11 + 2 * n, 0, 0, block, half, half)]
        groups.append((near + sides + far, plan, heads))
        col += cols
    return groups


def local(n_dp, tokens, ln_gain, w_qkv, q_gain, k_gain):
    heads_here = w_qkv.shape[1] // (3 * HD)
    depth = ln_gain.shape[0] // BLOCKS
    whole = lax.all_gather(tokens, "mp", axis=0)
    if n_dp == BLOCKS:
        sizes = [2] * (heads_here // 2) + [1] * (heads_here % 2)
        groups = square_groups(w_qkv, sizes)
        order = lax.axis_index("dp") ^ jnp.arange(BLOCKS, dtype=jnp.int32)
    else:
        full = lax.all_gather(w_qkv, "dp", axis=0, tiled=True)
        plan = [(0, m * depth, 0, m, 0, depth) for m in range(BLOCKS)]
        groups = [([full], plan, heads_here)]
        order = jnp.arange(BLOCKS, dtype=jnp.int32)
    normed = normalize(whole, ln_gain)
    parts = [attend(order, normed, sources, plan, q_gain, k_gain, heads) for sources, plan, heads in groups]
    return jnp.concatenate(parts, axis=1)


def solution(mesh):
    placed = (P("dp", "mp"), P(), P("dp", "mp"), P(), P())
    return jax.shard_map(
        functools.partial(local, mesh.shape["dp"]), mesh=mesh, in_specs=placed, out_specs=P("dp", "mp"), check_vma=False
    )
```

```python
import functools

import jax
import jax.numpy as jnp
from jax import lax
from jax.experimental import pallas as pl
from jax.experimental.pallas import tpu as pltpu
from jax.sharding import PartitionSpec as P

HD = 128
SEQ = 256
TILE = 256

eps = 1e-06

HBM = pl.BlockSpec(memory_space=pl.ANY)
VMEM = pl.BlockSpec(memory_space=pltpu.VMEM)
SMEM = pl.BlockSpec(memory_space=pltpu.SMEM)


def norm_last(values, gain):
    mean = jnp.mean(values, axis=-1, keepdims=True)
    square = jnp.mean(values * values, axis=-1, keepdims=True)
    return (values - mean) * lax.rsqrt(square - mean * mean + eps) * gain


def attend(acc, qg_ref, kg_ref, out_ref, heads):
    scale = 1.0 / HD**0.5
    for h in range(heads):
        base = 3 * HD * h
        query = norm_last(acc[:, base : base + HD], qg_ref[...]).astype(jnp.bfloat16)
        keyed = norm_last(acc[:, base + HD : base + 2 * HD], kg_ref[...]).astype(jnp.bfloat16)
        value = acc[:, base + 2 * HD : base + 3 * HD].astype(jnp.bfloat16)
        for i in range(acc.shape[0] // SEQ):
            rows = slice(i * SEQ, (i + 1) * SEQ)
            scores = lax.dot_general(
                query[rows], keyed[rows], (((1,), (1,)), ((), ())), preferred_element_type=jnp.float32
            ) * scale
            e = jnp.exp(scores - jnp.max(scores, axis=-1, keepdims=True))
            probs = (e / jnp.sum(e, axis=-1, keepdims=True)).astype(jnp.bfloat16)
            out_ref[rows, h * HD : (h + 1) * HD] = jnp.dot(
                probs, value[rows], preferred_element_type=jnp.float32
            ).astype(jnp.bfloat16)


def params():
    return pltpu.CompilerParams(vmem_limit_bytes=56 * 2**20)


def cost(rows, depth, cols, heads):
    return pl.CostEstimate(
        flops=2 * rows * depth * cols, bytes_accessed=2 * depth * (rows + cols), transcendentals=heads * rows * SEQ
    )


def copy_columns(source, col, target, row, sem):
    rows, cols = source.shape[0], target.shape[1]
    return pltpu.make_async_copy(source.at[:, pl.ds(col, cols)], target.at[pl.ds(row, rows)], sem)


def add_product(result, x_ref, w_ref):
    cols = w_ref.shape[1]
    tile = TILE if cols % TILE == 0 else HD

    @pl.loop(0, cols // tile)
    def _(t):
        lanes = pl.ds(pl.multiple_of(t * tile, tile), tile)
        result[:, lanes] += jnp.dot(x_ref[...], w_ref[:, lanes], preferred_element_type=jnp.float32)


def start_weights(entry, mask, pieces, col, core, w_all, sem):
    depth = w_all.shape[1] // 2
    for number, listed in pieces.items():

        @pl.when(mask == number)
        def _():
            for ref, base, other, row in listed:
                at = jnp.where(other == 0, core, 1 - core) * depth + row
                copy_columns(ref, col - base, w_all.at[entry], pl.multiple_of(at, 16), sem.at[entry]).start()


def wait_whole(ref, sem):
    pltpu.make_async_copy(ref, ref, sem).wait()


def near_kernel(table, steps, place_ref, *refs):
    normed, sources = refs[:steps], refs[steps:-5]
    out_ref, x_all, w_all, x_sem, w_sem = refs[-5:]
    line, chip, core = place_ref[0], place_ref[1], place_ref[2]
    pieces = {m: [(sources[n], *rest) for n, *rest in listed] for m, listed in table.items()}
    masks = [lax.rem(line - s + 4, 4) ^ chip for s in range(steps)]
    for s in range(steps):

        @pl.when(masks[s] != 3)
        def _():
            pltpu.make_async_copy(normed[s], x_all.at[s], x_sem.at[s]).start()

        start_weights(s, masks[s], pieces, 0, core, w_all, w_sem)
    out_ref[...] = jnp.zeros_like(out_ref)
    for s in range(steps):

        @pl.when(masks[s] != 3)
        def _():
            wait_whole(x_all.at[s], x_sem.at[s])
            wait_whole(w_all.at[s], w_sem.at[s])
            add_product(out_ref, x_all.at[s], w_all.at[s])


def near_sums(place, normed, sources, table, cols):
    steps = len(normed)
    rows, depth = normed[0].shape
    return pl.pallas_call(
        functools.partial(near_kernel, table, steps),
        in_specs=[SMEM] + [HBM] * (steps + len(sources)),
        out_specs=VMEM,
        out_shape=jax.ShapeDtypeStruct((rows, cols), jnp.float32),
        scratch_shapes=[
            pltpu.VMEM((steps, rows, depth), jnp.bfloat16),
            pltpu.VMEM((steps, depth, cols), jnp.bfloat16),
            pltpu.SemaphoreType.DMA((steps,)),
            pltpu.SemaphoreType.DMA((steps,)),
        ],
        compiler_params=params(),
        cost_estimate=cost(8, 128, cols, 0),
    )(place, *normed, *sources)


def last_kernel(table, first, heads, aliased, place_ref, qg_ref, kg_ref, sums_ref, *refs):
    normed, sources = refs[:4], refs[4 : -7 - aliased]
    out_ref, x_all, w_all, acc, x_sem, w_sem, a_sem = refs[-7:]
    line, chip, core = place_ref[0], place_ref[1], place_ref[2]
    pieces = {m: [(sources[n], *rest) for n, *rest in listed] for m, listed in table.items()}
    col = 3 * HD * first
    sums = pltpu.make_async_copy(sums_ref.at[:, pl.ds(col, acc.shape[1])], acc, a_sem)
    sums.start()
    mask = lax.rem(line + 1, 4) ^ chip

    @pl.when(mask != 3)
    def _():
        pltpu.make_async_copy(normed[3], x_all.at[0], x_sem.at[0]).start()
        start_weights(0, mask, {m: listed for m, listed in pieces.items() if m != 3}, col, core, w_all, w_sem)

    behind = lax.rem(line - (chip ^ 3) + 4, 4)
    for s in range(4):

        @pl.when(behind == s)
        def _():
            pltpu.make_async_copy(normed[s], x_all.at[1], x_sem.at[1]).start()

    start_weights(1, 3, {3: pieces[3]}, col, core, w_all, w_sem)
    sums.wait()

    @pl.when(mask != 3)
    def _():
        wait_whole(x_all.at[0], x_sem.at[0])
        wait_whole(w_all.at[0], w_sem.at[0])
        add_product(acc, x_all.at[0], w_all.at[0])

    wait_whole(x_all.at[1], x_sem.at[1])
    wait_whole(w_all.at[1], w_sem.at[1])
    add_product(acc, x_all.at[1], w_all.at[1])
    attend(acc, qg_ref, kg_ref, out_ref, heads)


def last_heads(place, normed, sums, sources, table, q_gain, k_gain, first, heads, all_heads, out):
    rows, depth = normed[0].shape
    cols = 3 * HD * heads
    previous = [] if out is None else [out]
    inputs = [place, q_gain.reshape(1, HD), k_gain.reshape(1, HD), sums, *normed, *sources, *previous]
    return pl.pallas_call(
        functools.partial(last_kernel, table, first, heads, len(previous)),
        grid=(1,),
        in_specs=[SMEM, VMEM, VMEM] + [HBM] * (len(inputs) - 3),
        out_specs=pl.BlockSpec((rows, HD * heads), lambda i: (0, first // heads)),
        out_shape=jax.ShapeDtypeStruct((rows, HD * all_heads), jnp.bfloat16),
        scratch_shapes=[
            pltpu.VMEM((2, rows, depth), jnp.bfloat16),
            pltpu.VMEM((2, depth, cols), jnp.bfloat16),
            pltpu.VMEM((rows, cols), jnp.float32),
            pltpu.SemaphoreType.DMA((2,)),
            pltpu.SemaphoreType.DMA((2,)),
            pltpu.SemaphoreType.DMA,
        ],
        input_output_aliases={len(inputs) - 1: 0} if previous else {},
        compiler_params=params(),
        cost_estimate=cost(8, 128, cols, heads),
    )(*inputs)


def swap(values, bit):
    return lax.ppermute(values, "dp", [(i, i ^ bit) for i in range(8)])


def ring(values, by=1):
    return lax.ppermute(values, "mp", [(i, (i + by) % 4) for i in range(4)])


def pair_sum(values, bit):
    return values + lax.ppermute(values, "mp", [(i, i ^ bit) for i in range(4)])


together = lax.optimization_barrier


def square_and_line(tokens, ln_gain, w, q_gain, k_gain):
    rows, width = tokens.shape
    cols = w.shape[1]
    all_heads = cols // (3 * HD)
    dp = lax.axis_index("dp")
    line = lax.axis_index("mp")
    place = jnp.stack([line, dp // 2, dp % 2]).astype(jnp.int32)

    half = w.shape[0] // 2
    top, low = w[:half], w[half:]
    x_low, y_top = swap(low, 2), swap(top, 4)
    z1 = ring(tokens)
    x_top, y_low = swap(top, 2), swap(low, 4)
    wide = tokens.astype(jnp.float32)
    stats = jnp.stack([jnp.sum(wide, axis=1), jnp.sum(wide * wide, axis=1)])
    pair = pair_sum(stats, 1)
    pair, z1 = together((pair, z1))
    total = pair_sum(pair, 2)
    z2 = ring(z1)
    sizes = [all_heads - all_heads // 3, all_heads // 3]
    cuts = [0, 3 * HD * sizes[0], cols]
    y_cut = [y_top[:, cuts[g] : cuts[g + 1]] for g in (0, 1)]
    x_cut = [x_low[:, cuts[g] : cuts[g + 1]] for g in (0, 1)]
    d0 = swap(y_cut[0], 2), swap(x_cut[0], 4)
    z3 = ring(z2)
    z2, x_low, y_top, x_top, y_low, total, w, y_cut, x_cut = together(
        (z2, x_low, y_top, x_top, y_low, total, w, y_cut, x_cut)
    )
    near, x_low_c, y_top_c, x_top_c, y_low_c = [swap(v, 1) for v in (w, x_low, y_top, x_top, y_low)]
    x_low_c, y_top_c, x_cut, y_cut = together((x_low_c, y_top_c, x_cut, y_cut))
    d1 = swap(y_cut[1], 2), swap(x_cut[1], 4)
    total = total / (4 * width)
    mean = total[0][:, None]
    scale = lax.rsqrt(total[1] - total[0] * total[0] + eps)[:, None]
    gains = ln_gain.reshape(4, 1, width)

    def normed(values, step):
        gain = lax.dynamic_index_in_dim(gains, (line - step + 4) % 4, keepdims=False)
        return ((values.astype(jnp.float32) - mean) * scale * gain).astype(jnp.bfloat16)

    sources = [w, near, x_top, x_low, x_top_c, x_low_c, y_top, y_low, y_top_c, y_low_c]
    table = {0: [(0, 0, 0, 0), (1, 0, 1, 0)]}
    for n, mask in enumerate((1, 2)):
        at = 2 + 4 * n
        table[mask] = [(at, 0, 0, 0), (at + 1, 0, 0, half), (at + 2, 0, 1, 0), (at + 3, 0, 1, half)]
    shards = [normed(tokens, 0), normed(z1, 1), normed(z2, 2)]
    sums = near_sums(place, shards, sources, table, cols)
    sums, z3 = together((sums, z3))
    shards.append(normed(z3, 3))
    out = None
    first = 0
    for heads, cut, far in zip(sizes, cuts, (d0, d1)):
        held = (sums if out is None else out, *far)
        held = together(held)
        sums, out = (held[0], None) if out is None else (sums, held[0])
        far = held[1:]
        far = [*far, swap(far[0], 1), swap(far[1], 1)]
        at = len(sources)
        here = {**table, 3: [(at, cut, 0, 0), (at + 1, cut, 0, half), (at + 2, cut, 1, 0), (at + 3, cut, 1, half)]}
        out = last_heads(place, shards, sums, sources + far, here, q_gain, k_gain, first, heads, all_heads, out)
        first += heads
    return out


def whole_kernel(qg_ref, kg_ref, x_ref, w_ref, out_ref, acc):
    acc[...] = jnp.zeros_like(acc)
    add_product(acc, x_ref, w_ref)
    attend(acc, qg_ref, kg_ref, out_ref, 1)


def gathered(tokens, ln_gain, w, q_gain, k_gain):
    whole = lax.all_gather(tokens, "mp", axis=1, tiled=True)
    normed = norm_last(whole.astype(jnp.float32), ln_gain).astype(jnp.bfloat16)
    full = lax.all_gather(w, "dp", axis=0, tiled=True)
    rows, depth = normed.shape
    cols = 3 * HD
    return pl.pallas_call(
        whole_kernel,
        grid=(w.shape[1] // cols, rows // SEQ),
        in_specs=[
            pl.BlockSpec((1, HD), lambda h, i: (0, 0)),
            pl.BlockSpec((1, HD), lambda h, i: (0, 0)),
            pl.BlockSpec((SEQ, depth), lambda h, i: (i, 0)),
            pl.BlockSpec((depth, cols), lambda h, i: (0, h)),
        ],
        out_specs=pl.BlockSpec((SEQ, HD), lambda h, i: (i, h)),
        out_shape=jax.ShapeDtypeStruct((rows, w.shape[1] // 3), jnp.bfloat16),
        scratch_shapes=[pltpu.VMEM((SEQ, cols), jnp.float32)],
        compiler_params=params(),
        cost_estimate=cost(rows, depth, w.shape[1], w.shape[1] // cols),
    )(q_gain.reshape(1, HD), k_gain.reshape(1, HD), normed, full)


def solution(mesh):
    placed = (P("dp", "mp"), P(), P("dp", "mp"), P(), P())
    square = mesh.shape["dp"] == 8 and mesh.shape["mp"] == 4
    return jax.shard_map(
        square_and_line if square else gathered,
        mesh=mesh, in_specs=placed, out_specs=P("dp", "mp"), check_vma=False,
    )
```

```python
import functools

import jax
import jax.numpy as jnp
from jax import lax
from jax.experimental import pallas as pl
from jax.experimental.pallas import tpu as pltpu
from jax.sharding import PartitionSpec as P

HD = 128
SEQ = 256
TILE = 256

eps = 1e-06

HBM = pl.BlockSpec(memory_space=pl.ANY)
VMEM = pl.BlockSpec(memory_space=pltpu.VMEM)
SMEM = pl.BlockSpec(memory_space=pltpu.SMEM)


def norm_last(values, gain):
    mean = jnp.mean(values, axis=-1, keepdims=True)
    square = jnp.mean(values * values, axis=-1, keepdims=True)
    return (values - mean) * lax.rsqrt(square - mean * mean + eps) * gain


def attend(acc, qg_ref, kg_ref, out_ref, heads):
    scale = 1.0 / HD**0.5
    for h in range(heads):
        base = 3 * HD * h
        query = norm_last(acc[:, base : base + HD], qg_ref[...]).astype(jnp.bfloat16)
        keyed = norm_last(acc[:, base + HD : base + 2 * HD], kg_ref[...]).astype(jnp.bfloat16)
        value = acc[:, base + 2 * HD : base + 3 * HD].astype(jnp.bfloat16)
        for i in range(acc.shape[0] // SEQ):
            rows = slice(i * SEQ, (i + 1) * SEQ)
            scores = lax.dot_general(
                query[rows], keyed[rows], (((1,), (1,)), ((), ())), preferred_element_type=jnp.float32
            ) * scale
            e = jnp.exp(scores - jnp.max(scores, axis=-1, keepdims=True))
            probs = (e / jnp.sum(e, axis=-1, keepdims=True)).astype(jnp.bfloat16)
            out_ref[rows, h * HD : (h + 1) * HD] = jnp.dot(
                probs, value[rows], preferred_element_type=jnp.float32
            ).astype(jnp.bfloat16)


def params():
    return pltpu.CompilerParams(vmem_limit_bytes=56 * 2**20)


def cost(rows, depth, cols, heads):
    return pl.CostEstimate(
        flops=2 * rows * depth * cols, bytes_accessed=2 * depth * (rows + cols), transcendentals=heads * rows * SEQ
    )


def add_product(result, x_ref, w_ref, fresh):
    cols = w_ref.shape[1]
    tile = TILE if cols % TILE == 0 else HD

    @pl.loop(0, cols // tile)
    def _(t):
        lanes = pl.ds(pl.multiple_of(t * tile, tile), tile)
        value = jnp.dot(x_ref[...], w_ref[:, lanes], preferred_element_type=jnp.float32)
        result[:, lanes] = value if fresh else result[:, lanes] + value


def start_weights(entry, mask, pieces, col, core, w_all, sem):
    depth = w_all.shape[1] // 2
    for number, listed in pieces.items():

        @pl.when(mask == number)
        def _():
            for ref, source_row, base, other, row, rows in listed:
                at = pl.multiple_of((1 - core if other else core) * depth + row, 16)
                pltpu.make_async_copy(
                    ref.at[pl.ds(source_row, rows), pl.ds(col - base, w_all.shape[2])],
                    w_all.at[entry, pl.ds(at, rows)],
                    sem.at[entry],
                ).start()


def wait_whole(ref, sem):
    pltpu.make_async_copy(ref, ref, sem).wait()


def unpack(table, place_ref, sources):
    return {m: [(sources[n], *rest) for n, *rest in listed] for m, listed in table.items()}


def early_kernel(table, count, place_ref, *refs):
    normed, sources = refs[:count], refs[count:-5]
    out_ref, x_all, w_all, x_sem, w_sem = refs[-5:]
    line, chip, core = place_ref[0], place_ref[1], place_ref[2]
    pieces = unpack(table, place_ref, sources)
    masks = [lax.rem(line - s + 4, 4) ^ chip for s in range(count)]

    def start(s):
        @pl.when(masks[s] != 3)
        def _():
            pltpu.make_async_copy(normed[s], x_all.at[s], x_sem.at[s]).start()

        start_weights(s, masks[s], pieces, 0, core, w_all, w_sem)

    start(0)
    out_ref[...] = jnp.zeros_like(out_ref)
    for s in range(count):
        if s + 1 < count:
            start(s + 1)

        @pl.when(masks[s] != 3)
        def _():
            wait_whole(x_all.at[s], x_sem.at[s])
            wait_whole(w_all.at[s], w_sem.at[s])
            add_product(out_ref, x_all.at[s], w_all.at[s], False)


def early_sums(place, normed, sources, table, cols):
    rows, depth = normed[0].shape
    count = len(normed)
    return pl.pallas_call(
        functools.partial(early_kernel, table, count),
        in_specs=[SMEM] + [HBM] * (count + len(sources)),
        out_specs=VMEM,
        out_shape=jax.ShapeDtypeStruct((rows, cols), jnp.float32),
        scratch_shapes=[
            pltpu.VMEM((count, rows, depth), jnp.bfloat16),
            pltpu.VMEM((count, depth, cols), jnp.bfloat16),
            pltpu.SemaphoreType.DMA((count,)),
            pltpu.SemaphoreType.DMA((count,)),
        ],
        compiler_params=params(),
        cost_estimate=cost(8, 128, cols, 0),
    )(place, *normed, *sources)


def last_kernel(table, first, heads, place_ref, qg_ref, kg_ref, sums_ref, *refs):
    normed, sources = refs[:4], refs[4:-7]
    out_ref, x_all, w_all, acc, x_sem, w_sem, a_sem = refs[-7:]
    line, chip, core = place_ref[0], place_ref[1], place_ref[2]
    pieces = unpack(table, place_ref, sources)
    diagonal = {3: pieces.pop(3)}
    col = 3 * HD * first
    mask = lax.rem(line + 1, 4) ^ chip
    behind = lax.rem(line - (chip ^ 3) + 4, 4)
    for s in range(4):

        @pl.when(behind == s)
        def _():
            pltpu.make_async_copy(normed[s], x_all.at[0], x_sem.at[0]).start()

    start_weights(0, 3, diagonal, col, core, w_all, w_sem)
    sums = pltpu.make_async_copy(sums_ref.at[:, pl.ds(col, acc.shape[1])], acc, a_sem)
    sums.start()
    sums.wait()
    wait_whole(x_all.at[0], x_sem.at[0])
    wait_whole(w_all.at[0], w_sem.at[0])

    @pl.when(mask != 3)
    def _():
        pltpu.make_async_copy(normed[3], x_all.at[1], x_sem.at[1]).start()
        start_weights(1, mask, pieces, col, core, w_all, w_sem)

    add_product(acc, x_all.at[0], w_all.at[0], False)

    @pl.when(mask != 3)
    def _():
        wait_whole(x_all.at[1], x_sem.at[1])
        wait_whole(w_all.at[1], w_sem.at[1])
        add_product(acc, x_all.at[1], w_all.at[1], False)

    attend(acc, qg_ref, kg_ref, out_ref, heads)


def last_heads(place, gains, normed, sums, sources, table, first, heads, all_heads, out=None):
    rows, depth = normed[0].shape
    cols = 3 * HD * heads
    previous = [] if out is None else [out]
    inputs = [place, *gains, sums, *normed, *sources, *previous]
    return pl.pallas_call(
        functools.partial(last_kernel, table, first, heads),
        grid=(1,),
        in_specs=[SMEM, VMEM, VMEM] + [HBM] * (len(inputs) - 3),
        out_specs=pl.BlockSpec((rows, HD * heads), lambda i: (0, first // heads)),
        out_shape=jax.ShapeDtypeStruct((rows, HD * all_heads), jnp.bfloat16),
        scratch_shapes=[
            pltpu.VMEM((2, rows, depth), jnp.bfloat16),
            pltpu.VMEM((2, depth, cols), jnp.bfloat16),
            pltpu.VMEM((rows, cols), jnp.float32),
            pltpu.SemaphoreType.DMA((2,)),
            pltpu.SemaphoreType.DMA((2,)),
            pltpu.SemaphoreType.DMA,
        ],
        input_output_aliases={len(inputs) - 1: 0} if previous else {},
        compiler_params=params(),
        cost_estimate=cost(8, 128, cols, heads),
    )(*inputs)


def swap(values, bit):
    return lax.ppermute(values, "dp", [(i, i ^ bit) for i in range(8)])


def ring(values, by=1):
    return lax.ppermute(values, "mp", [(i, (i + by) % 4) for i in range(4)])


def pair_sum(values, bit):
    return values + lax.ppermute(values, "mp", [(i, i ^ bit) for i in range(4)])


together = lax.optimization_barrier


def square_and_line(tokens, ln_gain, w, q_gain, k_gain):
    width = tokens.shape[1]
    cols = w.shape[1]
    all_heads = cols // (3 * HD)
    dp = lax.axis_index("dp")
    line = lax.axis_index("mp")
    place = jnp.stack([line, dp // 2, dp % 2]).astype(jnp.int32)
    half = w.shape[0] // 2

    top, low = w[:half], w[half:]
    x1, y1, z1, near = swap(low, 2), swap(top, 4), ring(tokens), swap(w, 1)
    wide = tokens.astype(jnp.float32)
    pair = pair_sum(jnp.stack([jnp.sum(wide, axis=1), jnp.sum(wide * wide, axis=1)]), 1)
    top, low, x1, y1, z1, near, pair = together((top, low, x1, y1, z1, near, pair))

    x2, y2, z2, x1_c, y1_c = swap(top, 2), swap(low, 4), ring(z1), swap(x1, 1), swap(y1, 1)
    total = pair_sum(pair, 2)
    x1, y1, x2, y2, z2, x1_c, y1_c, total = together((x1, y1, x2, y2, z2, x1_c, y1_c, total))

    x3, y3, z3, x2_c, y2_c = swap(y1, 2), swap(x1, 4), ring(z2), swap(x2, 1), swap(y2, 1)
    total = total / (4 * width)
    mean = total[0][:, None]
    scale = lax.rsqrt(total[1] - total[0] * total[0] + eps)[:, None]
    by_shard = ln_gain.reshape(4, 1, width)

    def normed(values, step):
        gain = lax.dynamic_index_in_dim(by_shard, (line - step + 4) % 4, keepdims=False)
        return ((values.astype(jnp.float32) - mean) * scale * gain).astype(jnp.bfloat16)

    held = [w, near, x1, x1_c, y1, y1_c, x2, x2_c, y2, y2_c]
    table = {0: [], 1: [], 2: [], 3: []}
    for other in (False, True):
        table[0].append((0 + other, 0, 0, other, 0, 2 * half))
        table[1] += [(2 + other, 0, 0, other, half, half), (6 + other, 0, 0, other, 0, half)]
        table[2] += [(4 + other, 0, 0, other, 0, half), (8 + other, 0, 0, other, half, half)]
        table[3] += [(10 + other, 0, 0, other, 0, half), (12 + other, 0, 0, other, half, half)]
    shards = [normed(tokens, 0), normed(z1, 1), normed(z2, 2)]
    sums = early_sums(place, shards, held, {m: table[m] for m in (0, 1, 2)}, cols)
    sums, x3, y3, z3 = together((sums, x3, y3, z3))
    held += [x3, swap(x3, 1), y3, swap(y3, 1)]
    shards.append(normed(z3, 3))
    gains = [q_gain.reshape(1, HD), k_gain.reshape(1, HD)]
    return last_heads(place, gains, shards, sums, held, table, 0, all_heads, all_heads)


def whole_kernel(qg_ref, kg_ref, x_ref, w_ref, out_ref, acc):
    add_product(acc, x_ref, w_ref, True)
    attend(acc, qg_ref, kg_ref, out_ref, 1)


def gathered(tokens, ln_gain, w, q_gain, k_gain):
    whole = lax.all_gather(tokens, "mp", axis=1, tiled=True)
    normed = norm_last(whole.astype(jnp.float32), ln_gain).astype(jnp.bfloat16)
    full = lax.all_gather(w, "dp", axis=0, tiled=True)
    rows, depth = normed.shape
    cols = 3 * HD
    return pl.pallas_call(
        whole_kernel,
        grid=(w.shape[1] // cols, rows // SEQ),
        in_specs=[
            pl.BlockSpec((1, HD), lambda h, i: (0, 0)),
            pl.BlockSpec((1, HD), lambda h, i: (0, 0)),
            pl.BlockSpec((SEQ, depth), lambda h, i: (i, 0)),
            pl.BlockSpec((depth, cols), lambda h, i: (0, h)),
        ],
        out_specs=pl.BlockSpec((SEQ, HD), lambda h, i: (i, h)),
        out_shape=jax.ShapeDtypeStruct((rows, w.shape[1] // 3), jnp.bfloat16),
        scratch_shapes=[pltpu.VMEM((SEQ, cols), jnp.float32)],
        compiler_params=params(),
        cost_estimate=cost(rows, depth, w.shape[1], w.shape[1] // cols),
    )(q_gain.reshape(1, HD), k_gain.reshape(1, HD), normed, full)


def solution(mesh):
    placed = (P("dp", "mp"), P(), P("dp", "mp"), P(), P())
    square = mesh.shape["dp"] == 8 and mesh.shape["mp"] == 4
    return jax.shard_map(
        square_and_line if square else gathered,
        mesh=mesh, in_specs=placed, out_specs=P("dp", "mp"), check_vma=False,
    )
```

```python
import functools

import jax
import jax.numpy as jnp
from jax import lax
from jax.experimental import pallas as pl
from jax.experimental.pallas import tpu as pltpu
from jax.sharding import PartitionSpec as P

HD = 128
SEQ = 256
TILE = 256

eps = 1e-06

HBM = pl.BlockSpec(memory_space=pl.ANY)
VMEM = pl.BlockSpec(memory_space=pltpu.VMEM)
SMEM = pl.BlockSpec(memory_space=pltpu.SMEM)


def norm_last(values, gain):
    mean = jnp.mean(values, axis=-1, keepdims=True)
    square = jnp.mean(values * values, axis=-1, keepdims=True)
    return (values - mean) * lax.rsqrt(square - mean * mean + eps) * gain


def attend(acc, qg_ref, kg_ref, out_ref, heads, first=0):
    scale = 1.0 / HD**0.5
    for h in range(heads):
        base = 3 * HD * h
        query = norm_last(acc[:, base : base + HD], qg_ref[...]).astype(jnp.bfloat16)
        keyed = norm_last(acc[:, base + HD : base + 2 * HD], kg_ref[...]).astype(jnp.bfloat16)
        value = acc[:, base + 2 * HD : base + 3 * HD].astype(jnp.bfloat16)
        for i in range(acc.shape[0] // SEQ):
            rows = slice(i * SEQ, (i + 1) * SEQ)
            scores = lax.dot_general(
                query[rows], keyed[rows], (((1,), (1,)), ((), ())), preferred_element_type=jnp.float32
            ) * scale
            e = jnp.exp(scores - jnp.max(scores, axis=-1, keepdims=True))
            probs = (e / jnp.sum(e, axis=-1, keepdims=True)).astype(jnp.bfloat16)
            out_ref[rows, (first + h) * HD : (first + h + 1) * HD] = jnp.dot(
                probs, value[rows], preferred_element_type=jnp.float32
            ).astype(jnp.bfloat16)


def params(mebibytes):
    return pltpu.CompilerParams(vmem_limit_bytes=mebibytes * 2**20)


def cost(rows, depth, cols, heads):
    return pl.CostEstimate(
        flops=2 * rows * depth * cols, bytes_accessed=2 * depth * (rows + cols), transcendentals=heads * rows * SEQ
    )


def add_product(result, before, x_ref, w_ref):
    cols = w_ref.shape[1]
    tile = TILE if cols % TILE == 0 else HD
    for t in range(0, cols, tile):
        lanes = slice(t, t + tile)
        value = jnp.dot(x_ref[...], w_ref[:, lanes], preferred_element_type=jnp.float32)
        result[:, lanes] = value if before is None else before[:, lanes] + value


def start_weights(entry, mask, pieces, col, core, w_all, sem):
    depth = w_all.shape[1] // 2
    for number, listed in pieces.items():

        @pl.when(mask == number)
        def _():
            for ref, source_row, base, other, row, rows in listed:
                at = pl.multiple_of((1 - core if other else core) * depth + row, 16)
                pltpu.make_async_copy(
                    ref.at[pl.ds(source_row, rows), pl.ds(col - base, w_all.shape[2])],
                    w_all.at[entry, pl.ds(at, rows)],
                    sem.at[entry],
                ).start()


def wait_whole(ref, sem):
    pltpu.make_async_copy(ref, ref, sem).wait()


def unpack(table, sources):
    return {m: [(sources[n], *rest) for n, *rest in listed] for m, listed in table.items()}


def early_kernel(table, count, col, ahead, place_ref, *refs):
    normed, sources = refs[:count], refs[count : -3 - ahead]
    out_ref, w_all, w_sem = refs[-3 - ahead], *refs[-2:]
    line, chip, core = place_ref[0], place_ref[1], place_ref[2]
    pieces = unpack(table, sources)
    masks = [lax.rem(line - s + 4, 4) ^ chip for s in range(count + 1)]

    def start(s):
        start_weights(s % 2, masks[s], pieces, col, core, w_all, w_sem.at[0])

    start(0)
    out_ref[...] = jnp.zeros_like(out_ref)
    for s in range(count):
        if s + 1 < count:
            start(s + 1)
        elif ahead:
            parts, _, cols = refs[-3].shape
            for part in range(parts):
                start_weights(part, masks[count], pieces, part * cols, core, refs[-3], w_sem.at[1])

        @pl.when(masks[s] != 3)
        def _():
            wait_whole(w_all.at[s % 2], w_sem.at[0, s % 2])
            add_product(out_ref, out_ref, normed[s], w_all.at[s % 2])

    if ahead:

        @pl.when(masks[count] != 3)
        def _():
            for part in range(refs[-3].shape[0]):
                wait_whole(refs[-3].at[part], w_sem.at[1, part])


def early_sums(place, normed, sources, table, col, cols, parts=0):
    rows, depth = normed[0].shape
    count = len(normed)
    out_shape = [jax.ShapeDtypeStruct((rows, cols), jnp.float32)]
    if parts:
        width = sources[0].shape[1] // parts
        out_shape.append(jax.ShapeDtypeStruct((parts, depth, width), jnp.bfloat16))
    return pl.pallas_call(
        functools.partial(early_kernel, table, count, col, len(out_shape) - 1),
        in_specs=[SMEM] + [VMEM] * count + [HBM] * len(sources),
        out_specs=[VMEM] * len(out_shape),
        out_shape=out_shape,
        scratch_shapes=[
            pltpu.VMEM((2, depth, cols), jnp.bfloat16),
            pltpu.SemaphoreType.DMA((2, max(2, parts))),
        ],
        compiler_params=params(20),
        cost_estimate=cost(8, 128, cols, 0),
    )(place, *normed, *sources)


def late_kernel(place_ref, x_ref, w_ref, *refs):
    before, after = refs[:2], refs[2:]
    parts, _, cols = w_ref.shape
    diagonal = lax.rem(place_ref[0] + 1, 4) ^ place_ref[1] == 3
    for ref, out_ref in zip(before, after):

        @pl.when(diagonal)
        def _():
            out_ref[...] = ref[...]

    @pl.when(jnp.logical_not(diagonal))
    def _():
        for part in range(parts):
            first = part * cols // before[0].shape[1]
            lanes = pl.ds(part * cols - first * before[0].shape[1], cols)
            add_product(after[first].at[:, lanes], before[first].at[:, lanes], x_ref, w_ref.at[part])


def late_sums(place, values, ahead, sums):
    return pl.pallas_call(
        late_kernel,
        in_specs=[SMEM] + [VMEM] * (2 + len(sums)),
        out_specs=[VMEM] * len(sums),
        out_shape=[jax.ShapeDtypeStruct(v.shape, v.dtype) for v in sums],
        compiler_params=params(8),
        cost_estimate=cost(8, 128, 128, 0),
    )(place, values, ahead, *sums)


def last_kernel(heads, split, place_ref, qg_ref, kg_ref, *refs):
    sums, normed, sources = refs[:2], refs[2:6], refs[6:10]
    out_ref, w_all, x_all, acc, w_sem, x_sem = refs[10:]
    parts, _, cols = w_all.shape
    line, chip, core = place_ref[0], place_ref[1], place_ref[2]
    behind = lax.rem(line - (chip ^ 3) + 4, 4)
    half = sources[0].shape[0]
    for s in range(4):

        @pl.when(behind == s)
        def _():
            pltpu.make_async_copy(normed[s], x_all, x_sem).start()

    for part in range(parts):
        for n, ref in enumerate(sources):
            at = pl.multiple_of((1 - core if n % 2 else core) * 2 * half + half * (n // 2), 16)
            pltpu.make_async_copy(
                ref.at[:, pl.ds(part * cols, cols)], w_all.at[part, pl.ds(at, half)], w_sem.at[part]
            ).start()
    wait_whole(x_all, x_sem)
    for part in range(parts):
        before = sums[0].at[:, pl.ds(part * cols, cols)] if part < split else sums[1]
        wait_whole(w_all.at[part], w_sem.at[part])
        add_product(acc.at[part], before, x_all, w_all.at[part])
        if part:
            attend(acc.at[part - 1], qg_ref, kg_ref, out_ref, heads, (part - 1) * heads)
    attend(acc.at[parts - 1], qg_ref, kg_ref, out_ref, heads, (parts - 1) * heads)


def last_heads(place, gains, normed, sums, sources, parts):
    rows, depth = normed[0].shape
    cols = sources[0].shape[1] // parts
    heads = cols // (3 * HD)
    inputs = [place, *gains, *sums, *normed, *sources]
    return pl.pallas_call(
        functools.partial(last_kernel, heads, sums[0].shape[1] // cols),
        in_specs=[SMEM] + [VMEM] * (len(inputs) - 1),
        out_specs=VMEM,
        out_shape=jax.ShapeDtypeStruct((rows, HD * heads * parts), jnp.bfloat16),
        scratch_shapes=[
            pltpu.VMEM((parts, depth, cols), jnp.bfloat16),
            pltpu.VMEM((rows, depth), jnp.bfloat16),
            pltpu.VMEM((parts, rows, cols), jnp.float32),
            pltpu.SemaphoreType.DMA((parts,)),
            pltpu.SemaphoreType.DMA,
        ],
        compiler_params=params(24),
        cost_estimate=cost(8, 128, cols, heads),
    )(*inputs)


def swap(values, bit):
    return lax.ppermute(values, "dp", [(i, i ^ bit) for i in range(8)])


def ring(values, by=1):
    return lax.ppermute(values, "mp", [(i, (i + by) % 4) for i in range(4)])


def pair_sum(values, bit):
    return values + lax.ppermute(values, "mp", [(i, i ^ bit) for i in range(4)])


together = lax.optimization_barrier


def square_and_line(tokens, ln_gain, w, q_gain, k_gain):
    width = tokens.shape[1]
    cols = w.shape[1]
    all_heads = cols // (3 * HD)
    dp = lax.axis_index("dp")
    line = lax.axis_index("mp")
    place = jnp.stack([line, dp // 2, dp % 2]).astype(jnp.int32)
    half = w.shape[0] // 2

    top, low = w[:half], w[half:]
    x1, y1, z1, near = swap(low, 2), swap(top, 4), ring(tokens), swap(w, 1)
    wide = tokens.astype(jnp.float32)
    pair = pair_sum(jnp.stack([jnp.sum(wide, axis=1), jnp.sum(wide * wide, axis=1)]), 1)
    top, low, x1, y1, z1, near, pair = together((top, low, x1, y1, z1, near, pair))

    sizes = [all_heads - all_heads // 3, all_heads // 3]
    cuts = [0, 3 * HD * sizes[0], cols]
    x2, y2, z2, x1_c, y1_c = swap(top, 2), swap(low, 4), ring(z1), swap(x1, 1), swap(y1, 1)
    pair, x1_c, y1_c = together((pair, x1_c, y1_c))
    total = pair_sum(pair, 2)
    x1, y1, x2, y2, z2, x1_c, y1_c, total = together((x1, y1, x2, y2, z2, x1_c, y1_c, total))

    x3, y3, z3, x2_c, y2_c = swap(y1, 2), swap(x1, 4), ring(z2), swap(x2, 1), swap(y2, 1)
    total = total / (4 * width)
    mean = total[0][:, None]
    scale = lax.rsqrt(total[1] - total[0] * total[0] + eps)[:, None]
    by_shard = ln_gain.reshape(4, 1, width)

    def normed(values, step):
        gain = lax.dynamic_index_in_dim(by_shard, (line - step + 4) % 4, keepdims=False)
        return ((values.astype(jnp.float32) - mean) * scale * gain).astype(jnp.bfloat16)

    held = [w, near, x1, x1_c, y1, y1_c, x2, x2_c, y2, y2_c]
    table = {0: [], 1: [], 2: []}
    for other in (False, True):
        table[0].append((0 + other, 0, 0, other, 0, 2 * half))
        table[1] += [(2 + other, 0, 0, other, half, half), (6 + other, 0, 0, other, 0, half)]
        table[2] += [(4 + other, 0, 0, other, 0, half), (8 + other, 0, 0, other, half, half)]
    shards = [normed(tokens, 0), normed(z1, 1), normed(z2, 2)]
    sums = early_sums(place, shards, held, table, 0, cuts[1])
    more, ahead = early_sums(place, shards, held, table, cuts[1], cols - cuts[1], 3)
    sums = [*sums, more]
    sums, ahead, x3, y3 = together((sums, ahead, x3, y3))
    far = [x3, swap(x3, 1), y3, swap(y3, 1)]
    sums, z3 = together((sums, z3))
    shards.append(normed(z3, 3))
    sums = late_sums(place, shards[3], ahead, sums)
    gains = [q_gain.reshape(1, HD), k_gain.reshape(1, HD)]
    return last_heads(place, gains, shards, sums, far, 3)


def whole_kernel(qg_ref, kg_ref, x_ref, w_ref, out_ref, acc):
    add_product(acc, None, x_ref, w_ref)
    attend(acc, qg_ref, kg_ref, out_ref, 1)


def gathered(tokens, ln_gain, w, q_gain, k_gain):
    whole = lax.all_gather(tokens, "mp", axis=1, tiled=True)
    normed = norm_last(whole.astype(jnp.float32), ln_gain).astype(jnp.bfloat16)
    full = lax.all_gather(w, "dp", axis=0, tiled=True)
    rows, depth = normed.shape
    cols = 3 * HD
    return pl.pallas_call(
        whole_kernel,
        grid=(w.shape[1] // cols, rows // SEQ),
        in_specs=[
            pl.BlockSpec((1, HD), lambda h, i: (0, 0)),
            pl.BlockSpec((1, HD), lambda h, i: (0, 0)),
            pl.BlockSpec((SEQ, depth), lambda h, i: (i, 0)),
            pl.BlockSpec((depth, cols), lambda h, i: (0, h)),
        ],
        out_specs=pl.BlockSpec((SEQ, HD), lambda h, i: (i, h)),
        out_shape=jax.ShapeDtypeStruct((rows, w.shape[1] // 3), jnp.bfloat16),
        scratch_shapes=[pltpu.VMEM((SEQ, cols), jnp.float32)],
        compiler_params=params(40),
        cost_estimate=cost(rows, depth, w.shape[1], w.shape[1] // cols),
    )(q_gain.reshape(1, HD), k_gain.reshape(1, HD), normed, full)


def solution(mesh):
    placed = (P("dp", "mp"), P(), P("dp", "mp"), P(), P())
    square = mesh.shape["dp"] == 8 and mesh.shape["mp"] == 4
    return jax.shard_map(
        square_and_line if square else gathered,
        mesh=mesh, in_specs=placed, out_specs=P("dp", "mp"), check_vma=False,
    )
```

```python
import functools

import jax
import jax.numpy as jnp
from jax import lax
from jax.experimental import pallas as pl
from jax.experimental.pallas import tpu as pltpu
from jax.sharding import PartitionSpec as P

HD = 128
SEQ = 256
TILE = 256

eps = 1e-06

HBM = pl.BlockSpec(memory_space=pl.ANY)
VMEM = pl.BlockSpec(memory_space=pltpu.VMEM)
SMEM = pl.BlockSpec(memory_space=pltpu.SMEM)


def norm_last(values, gain):
    mean = jnp.mean(values, axis=-1, keepdims=True)
    square = jnp.mean(values * values, axis=-1, keepdims=True)
    return (values - mean) * lax.rsqrt(square - mean * mean + eps) * gain


def attend(acc, qg_ref, kg_ref, out_ref, heads, first=0):
    scale = 1.0 / HD**0.5
    for h in range(heads):
        base = 3 * HD * h
        query = norm_last(acc[:, base : base + HD], qg_ref[...]).astype(jnp.bfloat16)
        keyed = norm_last(acc[:, base + HD : base + 2 * HD], kg_ref[...]).astype(jnp.bfloat16)
        value = acc[:, base + 2 * HD : base + 3 * HD].astype(jnp.bfloat16)
        for i in range(acc.shape[0] // SEQ):
            rows = slice(i * SEQ, (i + 1) * SEQ)
            scores = lax.dot_general(
                query[rows], keyed[rows], (((1,), (1,)), ((), ())), preferred_element_type=jnp.float32
            ) * scale
            e = jnp.exp(scores - jnp.max(scores, axis=-1, keepdims=True))
            probs = (e / jnp.sum(e, axis=-1, keepdims=True)).astype(jnp.bfloat16)
            out_ref[rows, (first + h) * HD : (first + h + 1) * HD] = jnp.dot(
                probs, value[rows], preferred_element_type=jnp.float32
            ).astype(jnp.bfloat16)


def params(mebibytes):
    return pltpu.CompilerParams(vmem_limit_bytes=mebibytes * 2**20)


def cost(rows, depth, cols, heads):
    return pl.CostEstimate(
        flops=2 * rows * depth * cols, bytes_accessed=2 * depth * (rows + cols), transcendentals=heads * rows * SEQ
    )


def add_product(result, before, x_ref, w_ref):
    cols = w_ref.shape[1]
    tile = TILE if cols % TILE == 0 else HD
    for t in range(0, cols, tile):
        lanes = slice(t, t + tile)
        value = jnp.dot(x_ref[...], w_ref[:, lanes], preferred_element_type=jnp.float32)
        result[:, lanes] = value if before is None else before[:, lanes] + value


def start_weights(entry, mask, pieces, col, core, w_all, sem):
    depth = w_all.shape[1] // 2
    for number, listed in pieces.items():

        @pl.when(mask == number)
        def _():
            for ref, source_row, base, other, row, rows in listed:
                at = pl.multiple_of((1 - core if other else core) * depth + row, 16)
                pltpu.make_async_copy(
                    ref.at[pl.ds(source_row, rows), pl.ds(col - base, w_all.shape[2])],
                    w_all.at[entry, pl.ds(at, rows)],
                    sem.at[entry],
                ).start()


def wait_whole(ref, sem):
    pltpu.make_async_copy(ref, ref, sem).wait()


def unpack(table, sources):
    return {m: [(sources[n], *rest) for n, *rest in listed] for m, listed in table.items()}


def early_kernel(table, count, col, ahead, place_ref, *refs):
    normed, sources = refs[:count], refs[count : -3 - ahead]
    out_ref, w_all, w_sem = refs[-3 - ahead], *refs[-2:]
    line, chip, core = place_ref[0], place_ref[1], place_ref[2]
    pieces = unpack(table, sources)
    masks = [lax.rem(line - s + 4, 4) ^ chip for s in range(count + 1)]

    def start(s):
        start_weights(s % 2, masks[s], pieces, col, core, w_all, w_sem.at[0])

    start(0)
    out_ref[...] = jnp.zeros_like(out_ref)
    for s in range(count):
        if s + 1 < count:
            start(s + 1)
        elif ahead:
            parts, _, cols = refs[-3].shape
            for part in range(parts):
                start_weights(part, masks[count], pieces, part * cols, core, refs[-3], w_sem.at[1])

        @pl.when(masks[s] != 3)
        def _():
            wait_whole(w_all.at[s % 2], w_sem.at[0, s % 2])
            add_product(out_ref, out_ref, normed[s], w_all.at[s % 2])

    if ahead:

        @pl.when(masks[count] != 3)
        def _():
            for part in range(refs[-3].shape[0]):
                wait_whole(refs[-3].at[part], w_sem.at[1, part])


def early_sums(place, normed, sources, table, col, cols, parts=0):
    rows, depth = normed[0].shape
    count = len(normed)
    out_shape = [jax.ShapeDtypeStruct((rows, cols), jnp.float32)]
    if parts:
        width = sources[0].shape[1] // parts
        out_shape.append(jax.ShapeDtypeStruct((parts, depth, width), jnp.bfloat16))
    return pl.pallas_call(
        functools.partial(early_kernel, table, count, col, len(out_shape) - 1),
        in_specs=[SMEM] + [VMEM] * count + [HBM] * len(sources),
        out_specs=[VMEM] * len(out_shape),
        out_shape=out_shape,
        scratch_shapes=[
            pltpu.VMEM((2, depth, cols), jnp.bfloat16),
            pltpu.SemaphoreType.DMA((2, max(2, parts))),
        ],
        compiler_params=params(13),
        cost_estimate=cost(8, 128, cols, 0),
    )(place, *normed, *sources)


def start_diagonal(place_ref, other, normed, sources, x_all, w_all, x_sem, w_sem):
    line, chip, core = place_ref[0], place_ref[1], place_ref[2]
    depth = x_all.shape[1]
    parts, _, cols = w_all.shape
    behind = lax.rem(line - (chip ^ 3) + 4, 4)
    features = pl.ds(pl.multiple_of((1 - core if other else core) * depth, depth), depth)
    for s in range(4):

        @pl.when(behind == s)
        def _():
            pltpu.make_async_copy(normed[s].at[:, features], x_all, x_sem).start()

    for part in range(parts):
        for n, ref in enumerate(sources):
            rows = ref.shape[0]
            pltpu.make_async_copy(
                ref.at[:, pl.ds(part * cols, cols)], w_all.at[part, pl.ds(n * rows, rows)], w_sem.at[part]
            ).start()


def part_of(sums, part, cols):
    first = part * cols // sums[0].shape[1]
    return sums[first].at[:, pl.ds(part * cols - first * sums[0].shape[1], cols)]


def late_kernel(place_ref, ahead_ref, x_ref, *refs):
    before, after = refs[:2], refs[2:4]
    parts, _, cols = ahead_ref.shape
    diagonal = lax.rem(place_ref[0] + 1, 4) ^ place_ref[1] == 3

    @pl.when(diagonal)
    def _():
        for ref, out_ref in zip(before, after):
            out_ref[...] = ref[...]

    @pl.when(jnp.logical_not(diagonal))
    def _():
        for part in range(parts):
            add_product(part_of(after, part, cols), part_of(before, part, cols), x_ref, ahead_ref.at[part])


def late_sums(place, values, ahead, sums):
    return pl.pallas_call(
        late_kernel,
        in_specs=[SMEM] + [VMEM] * (2 + len(sums)),
        out_specs=[VMEM] * len(sums),
        out_shape=[jax.ShapeDtypeStruct(v.shape, v.dtype) for v in sums],
        compiler_params=params(4),
        cost_estimate=cost(values.shape[0], values.shape[1], ahead.shape[0] * ahead.shape[2], 0),
    )(place, ahead, values, *sums)


def half_kernel(place_ref, *refs):
    normed, sources, before, after = refs[:4], refs[4:6], refs[6:8], refs[8:10]
    x_all, w_all, x_sem, w_sem = refs[10:]
    parts, _, cols = w_all.shape
    start_diagonal(place_ref, False, normed, sources, x_all, w_all, x_sem, w_sem)
    wait_whole(x_all, x_sem)
    for part in range(parts):
        wait_whole(w_all.at[part], w_sem.at[part])
        add_product(part_of(after, part, cols), part_of(before, part, cols), x_all, w_all.at[part])


def half_sums(place, normed, sources, sums, parts):
    rows, depth = normed[0].shape
    cols = sources[0].shape[1] // parts
    return pl.pallas_call(
        half_kernel,
        in_specs=[SMEM] + [VMEM] * (6 + len(sums)),
        out_specs=[VMEM] * len(sums),
        out_shape=[jax.ShapeDtypeStruct(v.shape, v.dtype) for v in sums],
        scratch_shapes=[
            pltpu.VMEM((rows, depth // 2), jnp.bfloat16),
            pltpu.VMEM((parts, depth // 2, cols), jnp.bfloat16),
            pltpu.SemaphoreType.DMA,
            pltpu.SemaphoreType.DMA((parts,)),
        ],
        compiler_params=params(7),
        cost_estimate=cost(8, 128, 128, 0),
    )(place, *normed, *sources, *sums)


def last_kernel(heads, place_ref, qg_ref, kg_ref, *refs):
    sums, normed, sources = refs[:2], refs[2:6], refs[6:8]
    out_ref, w_all, x_all, acc, w_sem, x_sem = refs[8:]
    parts, _, cols = w_all.shape
    start_diagonal(place_ref, True, normed, sources, x_all, w_all, x_sem, w_sem)
    wait_whole(x_all, x_sem)
    for part in range(parts):
        wait_whole(w_all.at[part], w_sem.at[part])
        add_product(acc.at[part], part_of(sums, part, cols), x_all, w_all.at[part])
        if part:
            attend(acc.at[part - 1], qg_ref, kg_ref, out_ref, heads, (part - 1) * heads)
    attend(acc.at[parts - 1], qg_ref, kg_ref, out_ref, heads, (parts - 1) * heads)


def last_heads(place, gains, normed, sums, sources, parts):
    rows, depth = normed[0].shape
    cols = sources[0].shape[1] // parts
    heads = cols // (3 * HD)
    inputs = [place, *gains, *sums, *normed, *sources]
    return pl.pallas_call(
        functools.partial(last_kernel, heads),
        in_specs=[SMEM] + [VMEM] * (len(inputs) - 1),
        out_specs=VMEM,
        out_shape=jax.ShapeDtypeStruct((rows, HD * heads * parts), jnp.bfloat16),
        scratch_shapes=[
            pltpu.VMEM((parts, depth // 2, cols), jnp.bfloat16),
            pltpu.VMEM((rows, depth // 2), jnp.bfloat16),
            pltpu.VMEM((parts, rows, cols), jnp.float32),
            pltpu.SemaphoreType.DMA((parts,)),
            pltpu.SemaphoreType.DMA,
        ],
        compiler_params=params(13),
        cost_estimate=cost(8, 128, cols, heads),
    )(*inputs)


def swap(values, bit):
    return lax.ppermute(values, "dp", [(i, i ^ bit) for i in range(8)])


def ring(values, by=1):
    return lax.ppermute(values, "mp", [(i, (i + by) % 4) for i in range(4)])


def pair_sum(values, bit):
    return values + lax.ppermute(values, "mp", [(i, i ^ bit) for i in range(4)])


together = lax.optimization_barrier


def square_and_line(tokens, ln_gain, w, q_gain, k_gain):
    width = tokens.shape[1]
    cols = w.shape[1]
    all_heads = cols // (3 * HD)
    dp = lax.axis_index("dp")
    line = lax.axis_index("mp")
    place = jnp.stack([line, dp // 2, dp % 2]).astype(jnp.int32)
    half = w.shape[0] // 2

    top, low = w[:half], w[half:]
    x1, y1, z1, near = swap(low, 2), swap(top, 4), ring(tokens), swap(w, 1)
    wide = tokens.astype(jnp.float32)
    pair = pair_sum(jnp.stack([jnp.sum(wide, axis=1), jnp.sum(wide * wide, axis=1)]), 1)
    top, low, x1, y1, z1, near, pair = together((top, low, x1, y1, z1, near, pair))

    sizes = [all_heads - all_heads // 3, all_heads // 3]
    cuts = [0, 3 * HD * sizes[0], cols]
    x2, y2, z2, x1_c, y1_c = swap(top, 2), swap(low, 4), ring(z1), swap(x1, 1), swap(y1, 1)
    pair, x1_c, y1_c = together((pair, x1_c, y1_c))
    total = pair_sum(pair, 2)
    x1, y1, x2, y2, z2, x1_c, y1_c, total = together((x1, y1, x2, y2, z2, x1_c, y1_c, total))

    x3, y3, z3, x2_c, y2_c = swap(y1, 2), swap(x1, 4), ring(z2), swap(x2, 1), swap(y2, 1)
    total = total / (4 * width)
    mean = total[0][:, None]
    scale = lax.rsqrt(total[1] - total[0] * total[0] + eps)[:, None]
    by_shard = ln_gain.reshape(4, 1, width)

    def normed(values, step):
        gain = lax.dynamic_index_in_dim(by_shard, (line - step + 4) % 4, keepdims=False)
        return ((values.astype(jnp.float32) - mean) * scale * gain).astype(jnp.bfloat16)

    held = [w, near, x1, x1_c, y1, y1_c, x2, x2_c, y2, y2_c]
    table = {0: [], 1: [], 2: []}
    for other in (False, True):
        table[0].append((0 + other, 0, 0, other, 0, 2 * half))
        table[1] += [(2 + other, 0, 0, other, half, half), (6 + other, 0, 0, other, 0, half)]
        table[2] += [(4 + other, 0, 0, other, 0, half), (8 + other, 0, 0, other, half, half)]
    shards = [normed(tokens, 0), normed(z1, 1), normed(z2, 2)]
    sums = early_sums(place, shards, held, table, 0, cuts[1])
    sums, shards = together((sums, shards))
    more, ahead = early_sums(place, shards, held, table, cuts[1], cols - cuts[1], 3)
    sums = [*sums, more]
    sums, ahead, z3 = together((sums, ahead, z3))
    shards.append(normed(z3, 3))
    sums = late_sums(place, shards[3], ahead, sums)
    sums, x3, y3 = together((sums, x3, y3))
    x3_c, y3_c = swap(x3, 1), swap(y3, 1)
    sums = half_sums(place, shards, [x3, y3], sums, 3)
    gains = [q_gain.reshape(1, HD), k_gain.reshape(1, HD)]
    return last_heads(place, gains, shards, sums, [x3_c, y3_c], 3)


def whole_kernel(qg_ref, kg_ref, x_ref, w_ref, out_ref, acc):
    add_product(acc, None, x_ref, w_ref)
    attend(acc, qg_ref, kg_ref, out_ref, 1)


def gathered(tokens, ln_gain, w, q_gain, k_gain):
    whole = lax.all_gather(tokens, "mp", axis=1, tiled=True)
    normed = norm_last(whole.astype(jnp.float32), ln_gain).astype(jnp.bfloat16)
    full = lax.all_gather(w, "dp", axis=0, tiled=True)
    rows, depth = normed.shape
    cols = 3 * HD
    return pl.pallas_call(
        whole_kernel,
        grid=(w.shape[1] // cols, rows // SEQ),
        in_specs=[
            pl.BlockSpec((1, HD), lambda h, i: (0, 0)),
            pl.BlockSpec((1, HD), lambda h, i: (0, 0)),
            pl.BlockSpec((SEQ, depth), lambda h, i: (i, 0)),
            pl.BlockSpec((depth, cols), lambda h, i: (0, h)),
        ],
        out_specs=pl.BlockSpec((SEQ, HD), lambda h, i: (i, h)),
        out_shape=jax.ShapeDtypeStruct((rows, w.shape[1] // 3), jnp.bfloat16),
        scratch_shapes=[pltpu.VMEM((SEQ, cols), jnp.float32)],
        compiler_params=params(40),
        cost_estimate=cost(rows, depth, w.shape[1], w.shape[1] // cols),
    )(q_gain.reshape(1, HD), k_gain.reshape(1, HD), normed, full)


def solution(mesh):
    placed = (P("dp", "mp"), P(), P("dp", "mp"), P(), P())
    square = mesh.shape["dp"] == 8 and mesh.shape["mp"] == 4
    return jax.shard_map(
        square_and_line if square else gathered,
        mesh=mesh, in_specs=placed, out_specs=P("dp", "mp"), check_vma=False,
    )
```

```python
import functools

import jax
import jax.numpy as jnp
from jax import lax
from jax.experimental import pallas as pl
from jax.experimental.pallas import tpu as pltpu
from jax.sharding import PartitionSpec as P

HD = 128
SEQ = 256
TILE = 256

eps = 1e-06

HBM = pl.BlockSpec(memory_space=pltpu.HBM)
VMEM = pl.BlockSpec(memory_space=pltpu.VMEM)
SMEM = pl.BlockSpec(memory_space=pltpu.SMEM)


def norm_last(values, gain):
    mean = jnp.mean(values, axis=-1, keepdims=True)
    square = jnp.mean(values * values, axis=-1, keepdims=True)
    return (values - mean) * lax.rsqrt(square - mean * mean + eps) * gain


def attend(acc, qg_ref, kg_ref, out_ref, heads, first=0):
    scale = 1.0 / HD**0.5
    for h in range(heads):
        base = 3 * HD * h
        query = norm_last(acc[:, base : base + HD], qg_ref[...]).astype(jnp.bfloat16)
        keyed = norm_last(acc[:, base + HD : base + 2 * HD], kg_ref[...]).astype(jnp.bfloat16)
        value = acc[:, base + 2 * HD : base + 3 * HD].astype(jnp.bfloat16)
        for i in range(acc.shape[0] // SEQ):
            rows = slice(i * SEQ, (i + 1) * SEQ)
            scores = lax.dot_general(
                query[rows], keyed[rows], (((1,), (1,)), ((), ())), preferred_element_type=jnp.float32
            ) * scale
            e = jnp.exp(scores - jnp.max(scores, axis=-1, keepdims=True))
            probs = (e / jnp.sum(e, axis=-1, keepdims=True)).astype(jnp.bfloat16)
            out_ref[rows, (first + h) * HD : (first + h + 1) * HD] = jnp.dot(
                probs, value[rows], preferred_element_type=jnp.float32
            ).astype(jnp.bfloat16)


def params(mebibytes):
    return pltpu.CompilerParams(vmem_limit_bytes=mebibytes * 2**20)


def cost(rows, depth, cols, heads):
    return pl.CostEstimate(
        flops=2 * rows * depth * cols, bytes_accessed=2 * depth * (rows + cols), transcendentals=heads * rows * SEQ
    )


def add_product(result, before, x_ref, w_ref):
    cols = w_ref.shape[1]
    tile = TILE if cols % TILE == 0 else HD
    for t in range(0, cols, tile):
        lanes = slice(t, t + tile)
        value = jnp.dot(x_ref[...], w_ref[:, lanes], preferred_element_type=jnp.float32)
        result[:, lanes] = value if before is None else before[:, lanes] + value


def start_weights(entry, mask, pieces, col, core, w_all, sem):
    depth = w_all.shape[1] // 2
    for number, listed in pieces.items():

        @pl.when(mask == number)
        def _():
            for ref, source_row, base, other, row, rows in listed:
                at = pl.multiple_of((1 - core if other else core) * depth + row, 16)
                pltpu.make_async_copy(
                    ref.at[pl.ds(source_row, rows), pl.ds(col - base, w_all.shape[2])],
                    w_all.at[entry, pl.ds(at, rows)],
                    sem.at[entry],
                ).start()


def wait_whole(ref, sem):
    pltpu.make_async_copy(ref, ref, sem).wait()


def unpack(table, sources):
    return {m: [(sources[n], *rest) for n, *rest in listed] for m, listed in table.items()}


def early_kernel(table, count, col, ahead, place_ref, *refs):
    normed, sources = refs[:count], refs[count : -3 - ahead]
    out_ref, w_all, w_sem = refs[-3 - ahead], *refs[-2:]
    line, chip, core = place_ref[0], place_ref[1], place_ref[2]
    pieces = unpack(table, sources)
    masks = [lax.rem(line - s + 4, 4) ^ chip for s in range(count + 1)]

    def start(s):
        start_weights(s % 2, masks[s], pieces, col, core, w_all, w_sem.at[0])

    start(0)
    out_ref[...] = jnp.zeros_like(out_ref)
    for s in range(count):
        if s + 1 < count:
            start(s + 1)
        elif ahead:
            parts, _, cols = refs[-3].shape
            for part in range(parts):
                start_weights(part, masks[count], pieces, part * cols, core, refs[-3], w_sem.at[1])

        @pl.when(masks[s] != 3)
        def _():
            wait_whole(w_all.at[s % 2], w_sem.at[0, s % 2])
            add_product(out_ref, out_ref, normed[s], w_all.at[s % 2])

    if ahead:

        @pl.when(masks[count] != 3)
        def _():
            for part in range(refs[-3].shape[0]):
                wait_whole(refs[-3].at[part], w_sem.at[1, part])


def early_sums(place, normed, sources, table, col, cols, parts=0):
    rows, depth = normed[0].shape
    count = len(normed)
    out_shape = [jax.ShapeDtypeStruct((rows, cols), jnp.float32)]
    if parts:
        width = sources[0].shape[1] // parts
        out_shape.append(jax.ShapeDtypeStruct((parts, depth, width), jnp.bfloat16))
    return pl.pallas_call(
        functools.partial(early_kernel, table, count, col, len(out_shape) - 1),
        in_specs=[SMEM] + [VMEM] * count + [HBM] * len(sources),
        out_specs=[VMEM] * len(out_shape),
        out_shape=out_shape,
        scratch_shapes=[
            pltpu.VMEM((2, depth, cols), jnp.bfloat16),
            pltpu.SemaphoreType.DMA((2, max(2, parts))),
        ],
        compiler_params=params(13),
        cost_estimate=cost(8, 128, cols, 0),
    )(place, *normed, *sources)


def start_diagonal(place_ref, other, normed, sources, x_all, w_all, x_sem, w_sem):
    line, chip, core = place_ref[0], place_ref[1], place_ref[2]
    depth = x_all.shape[1]
    parts, _, cols = w_all.shape
    behind = lax.rem(line - (chip ^ 3) + 4, 4)
    features = pl.ds(pl.multiple_of((1 - core if other else core) * depth, depth), depth)
    for s in range(4):

        @pl.when(behind == s)
        def _():
            pltpu.make_async_copy(normed[s].at[:, features], x_all, x_sem).start()

    for part in range(parts):
        for n, ref in enumerate(sources):
            rows = ref.shape[0]
            pltpu.make_async_copy(
                ref.at[:, pl.ds(part * cols, cols)], w_all.at[part, pl.ds(n * rows, rows)], w_sem.at[part]
            ).start()


def part_of(sums, part, cols):
    first = part * cols // sums[0].shape[1]
    return sums[first].at[:, pl.ds(part * cols - first * sums[0].shape[1], cols)]


def late_kernel(first, place_ref, ahead_ref, x_ref, before, after):
    cols = ahead_ref.shape[2]
    diagonal = lax.rem(place_ref[0] + 1, 4) ^ place_ref[1] == 3

    @pl.when(diagonal)
    def _():
        after[...] = before[...]

    @pl.when(jnp.logical_not(diagonal))
    def _():
        for part in range(before.shape[1] // cols):
            lanes = pl.ds(part * cols, cols)
            add_product(after.at[:, lanes], before.at[:, lanes], x_ref, ahead_ref.at[first + part])


def late_sums(place, values, ahead, sums, first):
    return pl.pallas_call(
        functools.partial(late_kernel, first),
        in_specs=[SMEM] + [VMEM] * 3,
        out_specs=VMEM,
        out_shape=jax.ShapeDtypeStruct(sums.shape, sums.dtype),
        compiler_params=params(4),
        cost_estimate=cost(values.shape[0], values.shape[1], sums.shape[1], 0),
    )(place, ahead, values, sums)


def half_kernel(place_ref, *refs):
    normed, sources, before, after = refs[:4], refs[4:6], refs[6:8], refs[8:10]
    x_all, w_all, x_sem, w_sem = refs[10:]
    parts, _, cols = w_all.shape
    start_diagonal(place_ref, False, normed, sources, x_all, w_all, x_sem, w_sem)
    wait_whole(x_all, x_sem)
    for part in range(parts):
        wait_whole(w_all.at[part], w_sem.at[part])
        add_product(part_of(after, part, cols), part_of(before, part, cols), x_all, w_all.at[part])


def half_sums(place, normed, sources, sums, parts):
    rows, depth = normed[0].shape
    cols = sources[0].shape[1] // parts
    return pl.pallas_call(
        half_kernel,
        in_specs=[SMEM] + [VMEM] * (6 + len(sums)),
        out_specs=[VMEM] * len(sums),
        out_shape=[jax.ShapeDtypeStruct(v.shape, v.dtype) for v in sums],
        scratch_shapes=[
            pltpu.VMEM((rows, depth // 2), jnp.bfloat16),
            pltpu.VMEM((parts, depth // 2, cols), jnp.bfloat16),
            pltpu.SemaphoreType.DMA,
            pltpu.SemaphoreType.DMA((parts,)),
        ],
        compiler_params=params(7),
        cost_estimate=cost(8, 128, 128, 0),
    )(place, *normed, *sources, *sums)


def last_kernel(heads, place_ref, qg_ref, kg_ref, *refs):
    sums, normed, sources = refs[:2], refs[2:6], refs[6:8]
    out_ref, w_all, x_all, acc, w_sem, x_sem = refs[8:]
    parts, _, cols = w_all.shape
    start_diagonal(place_ref, True, normed, sources, x_all, w_all, x_sem, w_sem)
    wait_whole(x_all, x_sem)
    for part in range(parts):
        wait_whole(w_all.at[part], w_sem.at[part])
        add_product(acc.at[part], part_of(sums, part, cols), x_all, w_all.at[part])
        if part:
            attend(acc.at[part - 1], qg_ref, kg_ref, out_ref, heads, (part - 1) * heads)
    attend(acc.at[parts - 1], qg_ref, kg_ref, out_ref, heads, (parts - 1) * heads)


def last_heads(place, gains, normed, sums, sources, parts):
    rows, depth = normed[0].shape
    cols = sources[0].shape[1] // parts
    heads = cols // (3 * HD)
    inputs = [place, *gains, *sums, *normed, *sources]
    return pl.pallas_call(
        functools.partial(last_kernel, heads),
        in_specs=[SMEM] + [VMEM] * (len(inputs) - 1),
        out_specs=VMEM,
        out_shape=jax.ShapeDtypeStruct((rows, HD * heads * parts), jnp.bfloat16),
        scratch_shapes=[
            pltpu.VMEM((parts, depth // 2, cols), jnp.bfloat16),
            pltpu.VMEM((rows, depth // 2), jnp.bfloat16),
            pltpu.VMEM((parts, rows, cols), jnp.float32),
            pltpu.SemaphoreType.DMA((parts,)),
            pltpu.SemaphoreType.DMA,
        ],
        compiler_params=params(13),
        cost_estimate=cost(8, 128, cols, heads),
    )(*inputs)


def swap(values, bit):
    return lax.ppermute(values, "dp", [(i, i ^ bit) for i in range(8)])


def ring(values, by=1):
    return lax.ppermute(values, "mp", [(i, (i + by) % 4) for i in range(4)])


def pair_sum(values, bit):
    return values + lax.ppermute(values, "mp", [(i, i ^ bit) for i in range(4)])


together = lax.optimization_barrier


def square_and_line(tokens, ln_gain, w, q_gain, k_gain):
    width = tokens.shape[1]
    cols = w.shape[1]
    all_heads = cols // (3 * HD)
    dp = lax.axis_index("dp")
    line = lax.axis_index("mp")
    place = jnp.stack([line, dp // 2, dp % 2]).astype(jnp.int32)
    half = w.shape[0] // 2

    top, low = w[:half], w[half:]
    x1, y1, z1, near = swap(low, 2), swap(top, 4), ring(tokens), swap(w, 1)
    wide = tokens.astype(jnp.float32)
    pair = pair_sum(jnp.stack([jnp.sum(wide, axis=1), jnp.sum(wide * wide, axis=1)]), 1)
    top, low, x1, y1, z1, near, pair = together((top, low, x1, y1, z1, near, pair))

    sizes = [all_heads - all_heads // 3, all_heads // 3]
    cuts = [0, 3 * HD * sizes[0], cols]
    x2, y2, z2, x1_c, y1_c = swap(top, 2), swap(low, 4), ring(z1), swap(x1, 1), swap(y1, 1)
    pair, x1_c, y1_c = together((pair, x1_c, y1_c))
    total = pair_sum(pair, 2)
    x1, y1, x2, y2, z2, x1_c, y1_c, total = together((x1, y1, x2, y2, z2, x1_c, y1_c, total))

    x3, y3, z3, x2_c, y2_c = swap(y1, 2), swap(x1, 4), ring(z2), swap(x2, 1), swap(y2, 1)
    total = total / (4 * width)
    mean = total[0][:, None]
    scale = lax.rsqrt(total[1] - total[0] * total[0] + eps)[:, None]
    x2_c, y2_c, by_shard = together((x2_c, y2_c, ln_gain.reshape(4, 1, width)))

    def normed(values, step):
        gain = lax.dynamic_index_in_dim(by_shard, (line - step + 4) % 4, keepdims=False)
        return ((values.astype(jnp.float32) - mean) * scale * gain).astype(jnp.bfloat16)

    held = [w, near, x1, x1_c, y1, y1_c, x2, x2_c, y2, y2_c]
    table = {0: [], 1: [], 2: []}
    for other in (False, True):
        table[0].append((0 + other, 0, 0, other, 0, 2 * half))
        table[1] += [(2 + other, 0, 0, other, half, half), (6 + other, 0, 0, other, 0, half)]
        table[2] += [(4 + other, 0, 0, other, 0, half), (8 + other, 0, 0, other, half, half)]
    shards = [normed(tokens, 0), normed(z1, 1), normed(z2, 2)]
    sums = early_sums(place, shards, held, table, 0, cuts[1])
    sums, shards = together((sums, shards))
    more, ahead = early_sums(place, shards, held, table, cuts[1], cols - cuts[1], 3)
    sums = [*sums, more]
    sums, ahead, z3 = together((sums, ahead, z3))
    shards.append(normed(z3, 3))
    split = sums[0].shape[1] // ahead.shape[2]
    sums[0] = late_sums(place, shards[3], ahead, sums[0], 0)
    sums, x3, y3 = together((sums, x3, y3))
    x3_c, y3_c = swap(x3, 1), swap(y3, 1)
    sums[1] = late_sums(place, shards[3], ahead, sums[1], split)
    sums = half_sums(place, shards, [x3, y3], sums, 3)
    gains = [q_gain.reshape(1, HD), k_gain.reshape(1, HD)]
    return last_heads(place, gains, shards, sums, [x3_c, y3_c], 3)


def whole_kernel(qg_ref, kg_ref, x_ref, w_ref, out_ref, acc):
    add_product(acc, None, x_ref, w_ref)
    attend(acc, qg_ref, kg_ref, out_ref, 1)


def gathered(tokens, ln_gain, w, q_gain, k_gain):
    whole = lax.all_gather(tokens, "mp", axis=1, tiled=True)
    normed = norm_last(whole.astype(jnp.float32), ln_gain).astype(jnp.bfloat16)
    full = lax.all_gather(w, "dp", axis=0, tiled=True)
    rows, depth = normed.shape
    cols = 3 * HD
    return pl.pallas_call(
        whole_kernel,
        grid=(w.shape[1] // cols, rows // SEQ),
        in_specs=[
            pl.BlockSpec((1, HD), lambda h, i: (0, 0)),
            pl.BlockSpec((1, HD), lambda h, i: (0, 0)),
            pl.BlockSpec((SEQ, depth), lambda h, i: (i, 0)),
            pl.BlockSpec((depth, cols), lambda h, i: (0, h)),
        ],
        out_specs=pl.BlockSpec((SEQ, HD), lambda h, i: (i, h)),
        out_shape=jax.ShapeDtypeStruct((rows, w.shape[1] // 3), jnp.bfloat16),
        scratch_shapes=[pltpu.VMEM((SEQ, cols), jnp.float32)],
        compiler_params=params(40),
        cost_estimate=cost(rows, depth, w.shape[1], w.shape[1] // cols),
    )(q_gain.reshape(1, HD), k_gain.reshape(1, HD), normed, full)


def solution(mesh):
    placed = (P("dp", "mp"), P(), P("dp", "mp"), P(), P())
    square = mesh.shape["dp"] == 8 and mesh.shape["mp"] == 4
    return jax.shard_map(
        square_and_line if square else gathered,
        mesh=mesh, in_specs=placed, out_specs=P("dp", "mp"), check_vma=False,
    )
```

```python
import functools

import jax
import jax.numpy as jnp
from jax import lax
from jax.experimental import pallas as pl
from jax.experimental.pallas import tpu as pltpu
from jax.sharding import PartitionSpec as P

HD = 128
SEQ = 256
TILE = 256

eps = 1e-06

HBM = pl.BlockSpec(memory_space=pltpu.HBM)
VMEM = pl.BlockSpec(memory_space=pltpu.VMEM)
SMEM = pl.BlockSpec(memory_space=pltpu.SMEM)


def norm_last(values, gain):
    mean = jnp.mean(values, axis=-1, keepdims=True)
    square = jnp.mean(values * values, axis=-1, keepdims=True)
    return (values - mean) * lax.rsqrt(square - mean * mean + eps) * gain


def attend(acc, qg_ref, kg_ref, out_ref, heads, first=0):
    scale = 1.0 / HD**0.5
    for h in range(heads):
        base = 3 * HD * h
        query = norm_last(acc[:, base : base + HD], qg_ref[...]).astype(jnp.bfloat16)
        keyed = norm_last(acc[:, base + HD : base + 2 * HD], kg_ref[...]).astype(jnp.bfloat16)
        value = acc[:, base + 2 * HD : base + 3 * HD].astype(jnp.bfloat16)
        for i in range(acc.shape[0] // SEQ):
            rows = slice(i * SEQ, (i + 1) * SEQ)
            scores = lax.dot_general(
                query[rows], keyed[rows], (((1,), (1,)), ((), ())), preferred_element_type=jnp.float32
            ) * scale
            e = jnp.exp(scores - jnp.max(scores, axis=-1, keepdims=True))
            probs = (e / jnp.sum(e, axis=-1, keepdims=True)).astype(jnp.bfloat16)
            out_ref[rows, (first + h) * HD : (first + h + 1) * HD] = jnp.dot(
                probs, value[rows], preferred_element_type=jnp.float32
            ).astype(jnp.bfloat16)


def params(mebibytes):
    return pltpu.CompilerParams(vmem_limit_bytes=mebibytes * 2**20)


def cost(rows, depth, cols, heads):
    return pl.CostEstimate(
        flops=2 * rows * depth * cols, bytes_accessed=2 * depth * (rows + cols), transcendentals=heads * rows * SEQ
    )


def add_product(result, before, x_ref, w_ref):
    cols = w_ref.shape[1]
    tile = TILE if cols % TILE == 0 else HD
    for t in range(0, cols, tile):
        lanes = slice(t, t + tile)
        value = jnp.dot(x_ref[...], w_ref[:, lanes], preferred_element_type=jnp.float32)
        result[:, lanes] = value if before is None else before[:, lanes] + value


def start_weights(entry, mask, pieces, col, core, w_all, sem):
    depth = w_all.shape[1] // 2
    for number, listed in pieces.items():

        @pl.when(mask == number)
        def _():
            for ref, source_row, base, other, row, rows in listed:
                at = pl.multiple_of((1 - core if other else core) * depth + row, 16)
                pltpu.make_async_copy(
                    ref.at[pl.ds(source_row, rows), pl.ds(col - base, w_all.shape[2])],
                    w_all.at[entry, pl.ds(at, rows)],
                    sem.at[entry],
                ).start()


def wait_whole(ref, sem):
    pltpu.make_async_copy(ref, ref, sem).wait()


def unpack(table, sources):
    return {m: [(sources[n], *rest) for n, *rest in listed] for m, listed in table.items()}


def early_kernel(table, count, col, ahead, place_ref, *refs):
    normed, sources = refs[:count], refs[count : -3 - ahead]
    out_ref, w_all, w_sem = refs[-3 - ahead], *refs[-2:]
    line, chip, core = place_ref[0], place_ref[1], place_ref[2]
    pieces = unpack(table, sources)
    masks = [lax.rem(line - s + 4, 4) ^ chip for s in range(count + 1)]

    def start(s):
        start_weights(s % 2, masks[s], pieces, col, core, w_all, w_sem.at[0])

    start(0)
    out_ref[...] = jnp.zeros_like(out_ref)
    for s in range(count):
        if s + 1 < count:
            start(s + 1)
        elif ahead:
            parts, _, cols = refs[-3].shape
            for part in range(parts):
                start_weights(part, masks[count], pieces, part * cols, core, refs[-3], w_sem.at[1])

        @pl.when(masks[s] != 3)
        def _():
            wait_whole(w_all.at[s % 2], w_sem.at[0, s % 2])
            add_product(out_ref, out_ref, normed[s], w_all.at[s % 2])

    if ahead:

        @pl.when(masks[count] != 3)
        def _():
            for part in range(refs[-3].shape[0]):
                wait_whole(refs[-3].at[part], w_sem.at[1, part])


def early_sums(place, normed, sources, table, col, cols, parts=0):
    rows, depth = normed[0].shape
    count = len(normed)
    out_shape = [jax.ShapeDtypeStruct((rows, cols), jnp.float32)]
    if parts:
        width = sources[0].shape[1] // parts
        out_shape.append(jax.ShapeDtypeStruct((parts, depth, width), jnp.bfloat16))
    return pl.pallas_call(
        functools.partial(early_kernel, table, count, col, len(out_shape) - 1),
        in_specs=[SMEM] + [VMEM] * count + [HBM] * len(sources),
        out_specs=[VMEM] * len(out_shape),
        out_shape=out_shape,
        scratch_shapes=[
            pltpu.VMEM((2, depth, cols), jnp.bfloat16),
            pltpu.SemaphoreType.DMA((2, max(2, parts))),
        ],
        compiler_params=params(13),
        cost_estimate=cost(8, 128, cols, 0),
    )(place, *normed, *sources)


def start_diagonal(place_ref, other, normed, sources, x_all, w_all, x_sem, w_sem):
    line, chip, core = place_ref[0], place_ref[1], place_ref[2]
    depth = x_all.shape[1]
    parts, _, cols = w_all.shape
    behind = lax.rem(line - (chip ^ 3) + 4, 4)
    features = pl.ds(pl.multiple_of((1 - core if other else core) * depth, depth), depth)
    for s in range(4):

        @pl.when(behind == s)
        def _():
            pltpu.make_async_copy(normed[s].at[:, features], x_all, x_sem).start()

    for part in range(parts):
        for n, ref in enumerate(sources):
            rows = ref.shape[0]
            pltpu.make_async_copy(
                ref.at[:, pl.ds(part * cols, cols)], w_all.at[part, pl.ds(n * rows, rows)], w_sem.at[part]
            ).start()


def part_of(sums, part, cols):
    first = part * cols // sums[0].shape[1]
    return sums[first].at[:, pl.ds(part * cols - first * sums[0].shape[1], cols)]


def late_kernel(first, place_ref, ahead_ref, x_ref, before, after):
    cols = ahead_ref.shape[2]
    diagonal = lax.rem(place_ref[0] + 1, 4) ^ place_ref[1] == 3

    @pl.when(diagonal)
    def _():
        after[...] = before[...]

    @pl.when(jnp.logical_not(diagonal))
    def _():
        for part in range(before.shape[1] // cols):
            lanes = pl.ds(part * cols, cols)
            add_product(after.at[:, lanes], before.at[:, lanes], x_ref, ahead_ref.at[first + part])


def late_sums(place, values, ahead, sums, first):
    return pl.pallas_call(
        functools.partial(late_kernel, first),
        in_specs=[SMEM] + [VMEM] * 3,
        out_specs=VMEM,
        out_shape=jax.ShapeDtypeStruct(sums.shape, sums.dtype),
        compiler_params=params(4),
        cost_estimate=cost(values.shape[0], values.shape[1], sums.shape[1], 0),
    )(place, ahead, values, sums)


def half_kernel(place_ref, *refs):
    normed, sources, before, after = refs[:4], refs[4:6], refs[6:8], refs[8:10]
    x_all, w_all, x_sem, w_sem = refs[10:]
    parts, _, cols = w_all.shape
    start_diagonal(place_ref, False, normed, sources, x_all, w_all, x_sem, w_sem)
    wait_whole(x_all, x_sem)
    for part in range(parts):
        wait_whole(w_all.at[part], w_sem.at[part])
        add_product(part_of(after, part, cols), part_of(before, part, cols), x_all, w_all.at[part])


def half_sums(place, normed, sources, sums, parts):
    rows, depth = normed[0].shape
    cols = sources[0].shape[1] // parts
    return pl.pallas_call(
        half_kernel,
        in_specs=[SMEM] + [VMEM] * (6 + len(sums)),
        out_specs=[VMEM] * len(sums),
        out_shape=[jax.ShapeDtypeStruct(v.shape, v.dtype) for v in sums],
        scratch_shapes=[
            pltpu.VMEM((rows, depth // 2), jnp.bfloat16),
            pltpu.VMEM((parts, depth // 2, cols), jnp.bfloat16),
            pltpu.SemaphoreType.DMA,
            pltpu.SemaphoreType.DMA((parts,)),
        ],
        compiler_params=params(7),
        cost_estimate=cost(8, 128, 128, 0),
    )(place, *normed, *sources, *sums)


def last_kernel(heads, place_ref, qg_ref, kg_ref, *refs):
    sums, normed, sources = refs[:2], refs[2:6], refs[6:8]
    out_ref, w_all, x_all, acc, w_sem, x_sem = refs[8:]
    parts, _, cols = w_all.shape
    start_diagonal(place_ref, True, normed, sources, x_all, w_all, x_sem, w_sem)
    wait_whole(x_all, x_sem)
    for part in range(parts):
        wait_whole(w_all.at[part], w_sem.at[part])
        add_product(acc.at[part], part_of(sums, part, cols), x_all, w_all.at[part])
        if part:
            attend(acc.at[part - 1], qg_ref, kg_ref, out_ref, heads, (part - 1) * heads)
    attend(acc.at[parts - 1], qg_ref, kg_ref, out_ref, heads, (parts - 1) * heads)


def last_heads(place, gains, normed, sums, sources, parts):
    rows, depth = normed[0].shape
    cols = sources[0].shape[1] // parts
    heads = cols // (3 * HD)
    inputs = [place, *gains, *sums, *normed, *sources]
    return pl.pallas_call(
        functools.partial(last_kernel, heads),
        in_specs=[SMEM] + [VMEM] * (len(inputs) - 1),
        out_specs=VMEM,
        out_shape=jax.ShapeDtypeStruct((rows, HD * heads * parts), jnp.bfloat16),
        scratch_shapes=[
            pltpu.VMEM((parts, depth // 2, cols), jnp.bfloat16),
            pltpu.VMEM((rows, depth // 2), jnp.bfloat16),
            pltpu.VMEM((parts, rows, cols), jnp.float32),
            pltpu.SemaphoreType.DMA((parts,)),
            pltpu.SemaphoreType.DMA,
        ],
        compiler_params=params(13),
        cost_estimate=cost(8, 128, cols, heads),
    )(*inputs)


def swap(values, bit):
    return lax.ppermute(values, "dp", [(i, i ^ bit) for i in range(8)])


def ring(values, by=1):
    return lax.ppermute(values, "mp", [(i, (i + by) % 4) for i in range(4)])


def pair_sum(values, bit):
    return values + lax.ppermute(values, "mp", [(i, i ^ bit) for i in range(4)])


together = lax.optimization_barrier


def square_and_line(tokens, ln_gain, w, q_gain, k_gain):
    width = tokens.shape[1]
    cols = w.shape[1]
    all_heads = cols // (3 * HD)
    dp = lax.axis_index("dp")
    line = lax.axis_index("mp")
    place = jnp.stack([line, dp // 2, dp % 2]).astype(jnp.int32)
    half = w.shape[0] // 2

    top, low = w[:half], w[half:]
    x1, y1, z1, near = swap(low, 2), swap(top, 4), ring(tokens), swap(w, 1)
    wide = tokens.astype(jnp.float32)
    pair = pair_sum(jnp.stack([jnp.sum(wide, axis=1), jnp.sum(wide * wide, axis=1)]), 1)
    z1, near, pair = together((z1, near, pair))

    sizes = [all_heads - all_heads // 3, all_heads // 3]
    cuts = [0, 3 * HD * sizes[0], cols]
    x2, y2, z2, x1_c, y1_c = swap(top, 2), swap(low, 4), ring(z1), swap(x1, 1), swap(y1, 1)
    pair, x1_c, y1_c = together((pair, x1_c, y1_c))
    total = pair_sum(pair, 2)
    x2, y2, z2, x1_c, y1_c, total = together((x2, y2, z2, x1_c, y1_c, total))

    x3, y3, z3, x2_c, y2_c = swap(y1, 2), swap(x1, 4), ring(z2), swap(x2, 1), swap(y2, 1)
    total = total / (4 * width)
    mean = total[0][:, None]
    scale = lax.rsqrt(total[1] - total[0] * total[0] + eps)[:, None]
    x2_c, y2_c, by_shard = together((x2_c, y2_c, ln_gain.reshape(4, 1, width)))

    def normed(values, step):
        gain = lax.dynamic_index_in_dim(by_shard, (line - step + 4) % 4, keepdims=False)
        return ((values.astype(jnp.float32) - mean) * scale * gain).astype(jnp.bfloat16)

    held = [w, near, x1, x1_c, y1, y1_c, x2, x2_c, y2, y2_c]
    table = {0: [], 1: [], 2: []}
    for other in (False, True):
        table[0].append((0 + other, 0, 0, other, 0, 2 * half))
        table[1] += [(2 + other, 0, 0, other, half, half), (6 + other, 0, 0, other, 0, half)]
        table[2] += [(4 + other, 0, 0, other, 0, half), (8 + other, 0, 0, other, half, half)]
    shards = [normed(tokens, 0), normed(z1, 1), normed(z2, 2)]
    sums = early_sums(place, shards, held, table, 0, cuts[1])
    sums, shards = together((sums, shards))
    more, ahead = early_sums(place, shards, held, table, cuts[1], cols - cuts[1], 3)
    sums = [*sums, more]
    sums, ahead, z3 = together((sums, ahead, z3))
    shards.append(normed(z3, 3))
    split = sums[0].shape[1] // ahead.shape[2]
    sums[0] = late_sums(place, shards[3], ahead, sums[0], 0)
    sums, x3, y3 = together((sums, x3, y3))
    x3_c, y3_c = swap(x3, 1), swap(y3, 1)
    sums[1] = late_sums(place, shards[3], ahead, sums[1], split)
    sums = half_sums(place, shards, [x3, y3], sums, 3)
    gains = [q_gain.reshape(1, HD), k_gain.reshape(1, HD)]
    return last_heads(place, gains, shards, sums, [x3_c, y3_c], 3)


def whole_kernel(qg_ref, kg_ref, x_ref, w_ref, out_ref, acc):
    add_product(acc, None, x_ref, w_ref)
    attend(acc, qg_ref, kg_ref, out_ref, 1)


def gathered(tokens, ln_gain, w, q_gain, k_gain):
    whole = lax.all_gather(tokens, "mp", axis=1, tiled=True)
    normed = norm_last(whole.astype(jnp.float32), ln_gain).astype(jnp.bfloat16)
    full = lax.all_gather(w, "dp", axis=0, tiled=True)
    rows, depth = normed.shape
    cols = 3 * HD
    return pl.pallas_call(
        whole_kernel,
        grid=(w.shape[1] // cols, rows // SEQ),
        in_specs=[
            pl.BlockSpec((1, HD), lambda h, i: (0, 0)),
            pl.BlockSpec((1, HD), lambda h, i: (0, 0)),
            pl.BlockSpec((SEQ, depth), lambda h, i: (i, 0)),
            pl.BlockSpec((depth, cols), lambda h, i: (0, h)),
        ],
        out_specs=pl.BlockSpec((SEQ, HD), lambda h, i: (i, h)),
        out_shape=jax.ShapeDtypeStruct((rows, w.shape[1] // 3), jnp.bfloat16),
        scratch_shapes=[pltpu.VMEM((SEQ, cols), jnp.float32)],
        compiler_params=params(40),
        cost_estimate=cost(rows, depth, w.shape[1], w.shape[1] // cols),
    )(q_gain.reshape(1, HD), k_gain.reshape(1, HD), normed, full)


def solution(mesh):
    placed = (P("dp", "mp"), P(), P("dp", "mp"), P(), P())
    square = mesh.shape["dp"] == 8 and mesh.shape["mp"] == 4
    return jax.shard_map(
        square_and_line if square else gathered,
        mesh=mesh, in_specs=placed, out_specs=P("dp", "mp"), check_vma=False,
    )
```

```python
import functools

import jax
import jax.numpy as jnp
from jax import lax
from jax.experimental import pallas as pl
from jax.experimental.pallas import tpu as pltpu
from jax.sharding import PartitionSpec as P

HD = 128
SEQ = 256
TILE = 256

eps = 1e-06

HBM = pl.BlockSpec(memory_space=pltpu.HBM)
VMEM = pl.BlockSpec(memory_space=pltpu.VMEM)
SMEM = pl.BlockSpec(memory_space=pltpu.SMEM)


def norm_last(values, gain):
    mean = jnp.mean(values, axis=-1, keepdims=True)
    square = jnp.mean(values * values, axis=-1, keepdims=True)
    return (values - mean) * lax.rsqrt(square - mean * mean + eps) * gain


def attend(acc, qg_ref, kg_ref, out_ref, heads, first=0):
    scale = 1.0 / HD**0.5
    for h in range(heads):
        base = 3 * HD * h
        query = norm_last(acc[:, base : base + HD], qg_ref[...]).astype(jnp.bfloat16)
        keyed = norm_last(acc[:, base + HD : base + 2 * HD], kg_ref[...]).astype(jnp.bfloat16)
        value = acc[:, base + 2 * HD : base + 3 * HD].astype(jnp.bfloat16)
        for i in range(acc.shape[0] // SEQ):
            rows = slice(i * SEQ, (i + 1) * SEQ)
            scores = lax.dot_general(
                query[rows], keyed[rows], (((1,), (1,)), ((), ())), preferred_element_type=jnp.float32
            ) * scale
            e = jnp.exp(scores - jnp.max(scores, axis=-1, keepdims=True))
            probs = (e / jnp.sum(e, axis=-1, keepdims=True)).astype(jnp.bfloat16)
            out_ref[rows, (first + h) * HD : (first + h + 1) * HD] = jnp.dot(
                probs, value[rows], preferred_element_type=jnp.float32
            ).astype(jnp.bfloat16)


def params(mebibytes):
    return pltpu.CompilerParams(vmem_limit_bytes=mebibytes * 2**20)


def cost(rows, depth, cols, heads):
    return pl.CostEstimate(
        flops=2 * rows * depth * cols, bytes_accessed=2 * depth * (rows + cols), transcendentals=heads * rows * SEQ
    )


def add_product(result, before, x_ref, w_ref):
    cols = w_ref.shape[1]
    tile = TILE if cols % TILE == 0 else HD
    for t in range(0, cols, tile):
        lanes = slice(t, t + tile)
        value = jnp.dot(x_ref[...], w_ref[:, lanes], preferred_element_type=jnp.float32)
        result[:, lanes] = value if before is None else before[:, lanes] + value


def start_weights(entry, mask, pieces, col, core, w_all, sem):
    depth = w_all.shape[1] // 2
    for number, listed in pieces.items():

        @pl.when(mask == number)
        def _():
            for ref, source_row, base, other, row, rows in listed:
                at = pl.multiple_of((1 - core if other else core) * depth + row, 16)
                pltpu.make_async_copy(
                    ref.at[pl.ds(source_row, rows), pl.ds(col - base, w_all.shape[2])],
                    w_all.at[entry, pl.ds(at, rows)],
                    sem.at[entry],
                ).start()


def wait_whole(ref, sem):
    pltpu.make_async_copy(ref, ref, sem).wait()


def unpack(table, sources):
    return {m: [(sources[n], *rest) for n, *rest in listed] for m, listed in table.items()}


def early_kernel(table, count, col, ahead, place_ref, *refs):
    normed, sources = refs[:count], refs[count : -3 - ahead]
    out_ref, w_all, w_sem = refs[-3 - ahead], *refs[-2:]
    line, chip, core = place_ref[0], place_ref[1], place_ref[2]
    pieces = unpack(table, sources)
    masks = [lax.rem(line - s + 4, 4) ^ chip for s in range(count + 1)]

    def start(s):
        start_weights(s % 2, masks[s], pieces, col, core, w_all, w_sem.at[0])

    start(0)
    out_ref[...] = jnp.zeros_like(out_ref)
    for s in range(count):
        if s + 1 < count:
            start(s + 1)
        elif ahead:
            parts, _, cols = refs[-3].shape
            for part in range(parts):
                start_weights(part, masks[count], pieces, part * cols, core, refs[-3], w_sem.at[1])

        @pl.when(masks[s] != 3)
        def _():
            wait_whole(w_all.at[s % 2], w_sem.at[0, s % 2])
            add_product(out_ref, out_ref, normed[s], w_all.at[s % 2])

    if ahead:

        @pl.when(masks[count] != 3)
        def _():
            for part in range(refs[-3].shape[0]):
                wait_whole(refs[-3].at[part], w_sem.at[1, part])


def early_sums(place, normed, sources, table, col, cols, parts=0):
    rows, depth = normed[0].shape
    count = len(normed)
    out_shape = [jax.ShapeDtypeStruct((rows, cols), jnp.float32)]
    if parts:
        width = sources[0].shape[1] // parts
        out_shape.append(jax.ShapeDtypeStruct((parts, depth, width), jnp.bfloat16))
    return pl.pallas_call(
        functools.partial(early_kernel, table, count, col, len(out_shape) - 1),
        in_specs=[SMEM] + [VMEM] * count + [HBM] * len(sources),
        out_specs=[VMEM] * len(out_shape),
        out_shape=out_shape,
        scratch_shapes=[
            pltpu.VMEM((2, depth, cols), jnp.bfloat16),
            pltpu.SemaphoreType.DMA((2, max(2, parts))),
        ],
        compiler_params=params(13),
        cost_estimate=cost(8, 128, cols, 0),
    )(place, *normed, *sources)


def start_features(place_ref, other, normed, x_all, sem):
    line, chip, core = place_ref[0], place_ref[1], place_ref[2]
    depth = x_all.shape[1]
    behind = lax.rem(line - (chip ^ 3) + 4, 4)
    features = pl.ds(pl.multiple_of((1 - core if other else core) * depth, depth), depth)
    for s in range(4):

        @pl.when(behind == s)
        def _():
            pltpu.make_async_copy(normed[s].at[:, features], x_all, sem).start()


def start_rows(sources, w_all, w_sem):
    parts, _, cols = w_all.shape
    for part in range(parts):
        for n, ref in enumerate(sources):
            rows = ref.shape[0]
            pltpu.make_async_copy(
                ref.at[:, pl.ds(part * cols, cols)], w_all.at[part, pl.ds(n * rows, rows)], w_sem.at[part]
            ).start()


def part_of(sums, part, cols):
    first = part * cols // sums[0].shape[1]
    return sums[first].at[:, pl.ds(part * cols - first * sums[0].shape[1], cols)]


def half_kernel(place_ref, ahead_ref, *refs):
    normed, sources, before, after = refs[:4], refs[4:6], refs[6:8], refs[8:10]
    x_next, x_all, w_all, x_sem, w_sem = refs[10:]
    diagonal = lax.rem(place_ref[0] + 1, 4) ^ place_ref[1] == 3
    parts, _, cols = w_all.shape
    start_features(place_ref, False, normed, x_all, x_sem.at[0])
    start_rows(sources, w_all, w_sem)
    start_features(place_ref, True, normed, x_next, x_sem.at[1])
    wait_whole(x_all, x_sem.at[0])
    for part in range(parts):
        wait_whole(w_all.at[part], w_sem.at[part])
        old, new = part_of(before, part, cols), part_of(after, part, cols)

        @pl.when(diagonal)
        def _():
            add_product(new, old, x_all, w_all.at[part])

        @pl.when(jnp.logical_not(diagonal))
        def _():
            for t in range(0, cols, TILE):
                lanes = slice(t, t + TILE)
                value = jnp.dot(normed[3][...], ahead_ref[part, :, lanes], preferred_element_type=jnp.float32)
                value += jnp.dot(x_all[...], w_all[part, :, lanes], preferred_element_type=jnp.float32)
                new[:, lanes] = old[:, lanes] + value

    wait_whole(x_next, x_sem.at[1])


def half_sums(place, ahead, normed, sources, sums, parts):
    rows, depth = normed[0].shape
    cols = sources[0].shape[1] // parts
    return pl.pallas_call(
        half_kernel,
        in_specs=[SMEM] + [VMEM] * (7 + len(sums)),
        out_specs=[VMEM] * (len(sums) + 1),
        out_shape=[jax.ShapeDtypeStruct(v.shape, v.dtype) for v in sums]
        + [jax.ShapeDtypeStruct((rows, depth // 2), jnp.bfloat16)],
        scratch_shapes=[
            pltpu.VMEM((rows, depth // 2), jnp.bfloat16),
            pltpu.VMEM((parts, depth // 2, cols), jnp.bfloat16),
            pltpu.SemaphoreType.DMA((2,)),
            pltpu.SemaphoreType.DMA((parts,)),
        ],
        compiler_params=params(7),
        cost_estimate=cost(8, 128, 128, 0),
    )(place, ahead, *normed, *sources, *sums)


def last_kernel(heads, place_ref, qg_ref, kg_ref, *refs):
    sums, x_ref, sources = refs[:2], refs[2], refs[3:5]
    out_ref, w_all, acc, w_sem = refs[5:]
    parts, _, cols = w_all.shape
    start_rows(sources, w_all, w_sem)
    for part in range(parts):
        wait_whole(w_all.at[part], w_sem.at[part])
        add_product(acc.at[part], part_of(sums, part, cols), x_ref, w_all.at[part])
        if part:
            attend(acc.at[part - 1], qg_ref, kg_ref, out_ref, heads, (part - 1) * heads)
    attend(acc.at[parts - 1], qg_ref, kg_ref, out_ref, heads, (parts - 1) * heads)


def last_heads(place, gains, features, sums, sources, parts):
    rows, depth = features.shape
    cols = sources[0].shape[1] // parts
    heads = cols // (3 * HD)
    inputs = [place, *gains, *sums, features, *sources]
    return pl.pallas_call(
        functools.partial(last_kernel, heads),
        in_specs=[SMEM] + [VMEM] * (len(inputs) - 1),
        out_specs=VMEM,
        out_shape=jax.ShapeDtypeStruct((rows, HD * heads * parts), jnp.bfloat16),
        scratch_shapes=[
            pltpu.VMEM((parts, depth, cols), jnp.bfloat16),
            pltpu.VMEM((parts, rows, cols), jnp.float32),
            pltpu.SemaphoreType.DMA((parts,)),
        ],
        compiler_params=params(13),
        cost_estimate=cost(8, 128, cols, heads),
    )(*inputs)


def swap(values, bit):
    return lax.ppermute(values, "dp", [(i, i ^ bit) for i in range(8)])


def ring(values, by=1):
    return lax.ppermute(values, "mp", [(i, (i + by) % 4) for i in range(4)])


def pair_sum(values, bit):
    return values + lax.ppermute(values, "mp", [(i, i ^ bit) for i in range(4)])


together = lax.optimization_barrier


def square_and_line(tokens, ln_gain, w, q_gain, k_gain):
    width = tokens.shape[1]
    cols = w.shape[1]
    all_heads = cols // (3 * HD)
    dp = lax.axis_index("dp")
    line = lax.axis_index("mp")
    place = jnp.stack([line, dp // 2, dp % 2]).astype(jnp.int32)
    half = w.shape[0] // 2

    top, low = w[:half], w[half:]
    x1, y1, z1, near = swap(low, 2), swap(top, 4), ring(tokens), swap(w, 1)
    wide = tokens.astype(jnp.float32)
    pair = pair_sum(jnp.stack([jnp.sum(wide, axis=1), jnp.sum(wide * wide, axis=1)]), 1)
    z1, near, pair = together((z1, near, pair))

    sizes = [all_heads - all_heads // 3, all_heads // 3]
    cuts = [0, 3 * HD * sizes[0], cols]
    x2, y2, z2, x1_c, y1_c = swap(top, 2), swap(low, 4), ring(z1), swap(x1, 1), swap(y1, 1)
    pair, x1_c, y1_c = together((pair, x1_c, y1_c))
    total = pair_sum(pair, 2)
    x2, y2, z2, x1_c, y1_c, total = together((x2, y2, z2, x1_c, y1_c, total))

    x3, y3, z3, x2_c, y2_c = swap(y1, 2), swap(x1, 4), ring(z2), swap(x2, 1), swap(y2, 1)
    total = total / (4 * width)
    mean = total[0][:, None]
    scale = lax.rsqrt(total[1] - total[0] * total[0] + eps)[:, None]
    x2_c, y2_c, by_shard = together((x2_c, y2_c, ln_gain.reshape(4, 1, width)))

    def normed(values, step):
        gain = lax.dynamic_index_in_dim(by_shard, (line - step + 4) % 4, keepdims=False)
        return ((values.astype(jnp.float32) - mean) * scale * gain).astype(jnp.bfloat16)

    held = [w, near, x1, x1_c, y1, y1_c, x2, x2_c, y2, y2_c]
    table = {0: [], 1: [], 2: []}
    for other in (False, True):
        table[0].append((0 + other, 0, 0, other, 0, 2 * half))
        table[1] += [(2 + other, 0, 0, other, half, half), (6 + other, 0, 0, other, 0, half)]
        table[2] += [(4 + other, 0, 0, other, 0, half), (8 + other, 0, 0, other, half, half)]
    shards = [normed(tokens, 0), normed(z1, 1), normed(z2, 2)]
    sums = early_sums(place, shards, held, table, 0, cuts[1])
    sums, shards = together((sums, shards))
    more, ahead = early_sums(place, shards, held, table, cuts[1], cols - cuts[1], 3)
    sums = [*sums, more]
    sums, ahead, z3 = together((sums, ahead, z3))
    shards.append(normed(z3, 3))
    shards, x3, y3 = together((shards, x3, y3))
    x3_c, y3_c = swap(x3, 1), swap(y3, 1)
    *sums, features = half_sums(place, ahead, shards, [x3, y3], sums, 3)
    gains = [q_gain.reshape(1, HD), k_gain.reshape(1, HD)]
    return last_heads(place, gains, features, sums, [x3_c, y3_c], 3)


def whole_kernel(qg_ref, kg_ref, x_ref, w_ref, out_ref, acc):
    add_product(acc, None, x_ref, w_ref)
    attend(acc, qg_ref, kg_ref, out_ref, 1)


def gathered(tokens, ln_gain, w, q_gain, k_gain):
    whole = lax.all_gather(tokens, "mp", axis=1, tiled=True)
    normed = norm_last(whole.astype(jnp.float32), ln_gain).astype(jnp.bfloat16)
    full = lax.all_gather(w, "dp", axis=0, tiled=True)
    rows, depth = normed.shape
    cols = 3 * HD
    return pl.pallas_call(
        whole_kernel,
        grid=(w.shape[1] // cols, rows // SEQ),
        in_specs=[
            pl.BlockSpec((1, HD), lambda h, i: (0, 0)),
            pl.BlockSpec((1, HD), lambda h, i: (0, 0)),
            pl.BlockSpec((SEQ, depth), lambda h, i: (i, 0)),
            pl.BlockSpec((depth, cols), lambda h, i: (0, h)),
        ],
        out_specs=pl.BlockSpec((SEQ, HD), lambda h, i: (i, h)),
        out_shape=jax.ShapeDtypeStruct((rows, w.shape[1] // 3), jnp.bfloat16),
        scratch_shapes=[pltpu.VMEM((SEQ, cols), jnp.float32)],
        compiler_params=params(40),
        cost_estimate=cost(rows, depth, w.shape[1], w.shape[1] // cols),
    )(q_gain.reshape(1, HD), k_gain.reshape(1, HD), normed, full)


def solution(mesh):
    placed = (P("dp", "mp"), P(), P("dp", "mp"), P(), P())
    square = mesh.shape["dp"] == 8 and mesh.shape["mp"] == 4
    return jax.shard_map(
        square_and_line if square else gathered,
        mesh=mesh, in_specs=placed, out_specs=P("dp", "mp"), check_vma=False,
    )
```
